32 devices in a mesh: ctx: 4 (over x, core), tp: 8 (over z, y).
Axes of the slice: x: 2, y: 2, z: 4, core: 2. Of those that a mesh axis runs over, the one named last changes fastest.
Arguments:
- queries: bfloat16 [512, 3072], P('ctx', 'tp'), may hold values from -80 to 80
- key_rows: bfloat16 [512, 512], P('ctx'), may hold values from -4 to 4
- value_rows: bfloat16 [512, 512], P('ctx'), may hold values from -6 to 6
- out_grad: bfloat16 [512, 3072], P('ctx', 'tp'), may hold values from -6 to 6
- attn_out: bfloat16 [512, 3072], P('ctx', 'tp'), may hold values from -6 to 6
- doc_ids: int32 [512], replicated, may hold values from 0 to 7, never falling along the last dimension, each value on 1 to 384 neighbouring positions
- row_grad: bfloat16 [512, 6144], P('ctx', 'tp'), may hold values from -6 to 6
- gate_weights: float32 [512, 2], P('ctx'), may hold values from 0.1 to 0.9
- expert_ids: int32 [512, 2], P('ctx'), may hold values from 0 to 3, all different within a row; in each aligned block of 128 rows (0 to 127, 128 to 255, ...) at most 128 rows name the same one
- expert_out: bfloat16 [4, 512, 6144], P('ctx', 'tp'), may hold values from -0.079589844 to 0.079589844
Outputs:
- query_grad: bfloat16 [512, 3072], P('ctx', 'tp')
- key_grad: bfloat16 [512, 512], P('ctx', 'tp')
- value_grad: bfloat16 [512, 512], P('ctx', 'tp')
- gate_grad: float32 [4, 512], P('ctx', 'tp')
- expert_grad: bfloat16 [4, 512, 6144], P('ctx', 'tp')
The draws below stay inside these ranges and needn't reach their ends.
Inputs may be any that keep to these rules, and one draw needn't show every extreme that they name: `doc_ids`: never falling along the tokens; each document holds 1 to 384 tokens and one holds exactly 384. `expert_ids`: A token's 2 experts differ; within each aligned block of 128 tokens no expert is named by more than 128 entries, and in some block an expert is named by exactly 128.
All inputs are finite; a program needn't handle non-finite values.
Results may differ from the reference program's by a relative error of at most 0.006.
Values may be sent and summed in bfloat16 or wider, within the bound.
A program may use at most 64 MiB of HBM per device.

```python
import math
import jax
import jax.numpy as jnp
import numpy as np
from jax import lax

D = 6144
HD = 128
TOP = 2
DOCS = 8
TOK_DEV = 128
H = 24
KVH = 4
EXPERTS = 4
TOKENS = 512
DOC_MAX = 384
CAP_E = 128
CAP = 64
GROUPS = 4


def raw_keys(key):
    return jnp.clip(jax.random.normal(jax.random.fold_in(key, 11), (TOKENS, KVH * HD), jnp.float32), -4.0, 4.0)


def draw_key_rows(key, part):
    return raw_keys(key).astype(jnp.bfloat16)


def draw_queries(key, part):
    base_queries = jnp.clip(jax.random.normal(jax.random.fold_in(key, 23), (TOKENS, H * HD), jnp.float32), -6.0, 6.0)
    return base_queries.astype(jnp.bfloat16)


def block_levels(key, dims, cuts, least, high):
    level = 1.0
    for dim, shards_of in cuts:
        draws = jax.random.uniform(jax.random.fold_in(jax.random.fold_in(key, 6), dim), (shards_of,), jnp.float32, least / len(cuts), high / len(cuts))
        level = level * jnp.repeat(jnp.exp(draws), dims[dim] // shards_of).reshape((-1,) + (1,) * (len(dims) - 1 - dim))
    return level


def profile(number_of, total, most, slope):
    portions = [(1 << 20) // math.isqrt(grade ** slope) + 1 for grade in range(2, number_of + 1)]
    spare, holding = total - most - (number_of - 1), [1] * (number_of - 1)
    while spare > 0:
        free = [i for i in range(number_of - 1) if holding[i] < most]
        whole, remaining = sum([portions[i] for i in free]), spare
        for i in free:
            more = min(most - holding[i], max(1, remaining * portions[i] // whole), spare)
            holding[i] = holding[i] + more
            spare = spare - more
    return np.array([most] + holding)


def ragged(own_key, number_of, total, reach, slope):
    if number_of == 2:
        one = jax.random.randint(own_key, (), max(1, total - reach), min(reach, total - 1) + 1)
        return jnp.stack([one, total - one])
    tallies = jnp.asarray(profile(number_of, total, reach, slope), jnp.int32)
    couples = (number_of - 1) // 2
    giver, taker = tallies[1:1 + 2 * couples:2], tallies[2:2 + 2 * couples:2]
    room = jnp.minimum(giver - 1, reach - taker)
    moved = jax.random.randint(jax.random.fold_in(own_key, 1), (couples,), 0, 1 << 20) % (room + 1)
    tallies = tallies.at[1:1 + 2 * couples:2].set(giver - moved).at[2:2 + 2 * couples:2].set(taker + moved)
    return tallies[jax.random.permutation(jax.random.fold_in(own_key, 2), number_of)]


def shared_out(own_key, own, number, rows, amount, top, bound, slope):
    order = jax.random.permutation(own_key, amount)
    crowded, common = portions_of(amount, rows * top, bound, slope, True), portions_of(amount, rows * top, bound, slope, False)
    places = jnp.arange(amount)

    def named(tallies, offset_by):
        used = int((tallies > 0).sum())
        fixed = max(1, used // 4)
        passed = fixed + (places - fixed + offset_by * (used - fixed)) % max(1, amount - fixed)
        return jnp.zeros((amount,), jnp.int32).at[order[jnp.where(places < fixed, places, passed)]].set(jnp.asarray(tallies, jnp.int32))

    tallies = jnp.where(number % 4 == 0, named(crowded, number // 4), named(common, number - number // 4 - 1))
    mixed = jax.random.permutation(jax.random.fold_in(own, 3), amount)
    donor, receiver = mixed[0:amount // 2 * 2:2], mixed[1:amount // 2 * 2:2]
    room = jnp.minimum(tallies[donor] - 1, bound - tallies[receiver]) // 2
    room = jnp.where((donor == order[0]) | (receiver == order[0]) | (tallies[receiver] == 0), 0, jnp.maximum(room, 0))
    passed = jax.random.randint(jax.random.fold_in(own, 4), (amount // 2,), 0, 1 << 20) % (room + 1)
    tallies = tallies.at[donor].add(-passed).at[receiver].add(passed)
    items = jnp.searchsorted(jnp.cumsum(tallies), jnp.arange(rows * top), side="right").astype(jnp.int32)
    table = items.reshape(top, rows).T
    table = table[jax.random.permutation(jax.random.fold_in(own, 1), rows)]
    offset_by = jax.random.randint(jax.random.fold_in(own, 2), (rows, 1), 0, top)
    return jnp.take_along_axis(table, (jnp.arange(top)[None, :] + offset_by) % top, axis=1)


def portions_of(amount, total, reach, lean, full):
    weights = [(1 << 20) // math.isqrt(standing ** lean) + 1 for standing in range(1, amount + 1)]
    largest = reach if full else min(reach, max(-(-total // amount), total * weights[0] // sum(weights)))
    least = 1 if total - largest >= amount - 1 else 0
    counts, rest = [largest] + [least] * (amount - 1), total - largest - least * (amount - 1)
    while rest > 0:
        movable = [i for i in range(1, amount) if counts[i] < largest] or [i for i in range(1, amount) if counts[i] < reach]
        pool, remaining = sum([weights[i] for i in movable]), rest
        for i in movable:
            extra = min(reach - counts[i], max(1, remaining * weights[i] // pool), rest)
            counts[i] = counts[i] + extra
            rest = rest - extra
    return np.array(counts)


def bell_draw(key, extent, width, reach, split=(), kind=jnp.bfloat16):
    drawn = width * jax.random.normal(key, extent, jnp.float32)
    if split:
        drawn = drawn * block_levels(key, extent, split, -0.22, 0.18)
    return jnp.clip(drawn, -reach, reach).astype(kind)


def setup_inputs(seed: int = 0) -> dict:
    seeds = jax.random.split(jax.random.key(seed), 11)
    queries = draw_queries(jax.random.fold_in(seeds[10], 71), 0)
    key_rows = draw_key_rows(jax.random.fold_in(seeds[10], 71), 0)
    value_rows = bell_draw(seeds[2], (TOKENS, KVH * HD), 1.0, 6.0, ((0, 4),))
    out_grad = bell_draw(seeds[3], (TOKENS, H * HD), 1.0, 6.0, ((0, 4), (1, 8)))
    attn_out = bell_draw(seeds[4], (TOKENS, H * HD), 1.0, 6.0, ((0, 4), (1, 8)))
    doc_ids = jnp.searchsorted(jnp.cumsum(ragged(seeds[5], DOCS, TOKENS, DOC_MAX, 2)), jnp.arange(TOKENS), side="right").astype(jnp.int32)
    row_grad = bell_draw(seeds[6], (TOKENS, D), 1.0, 6.0, ((0, 4), (1, 8)))
    gate_weights = jnp.clip(0.1 + 0.79999997 * jax.random.uniform(seeds[7], (TOKENS, TOP), jnp.float32) ** block_levels(seeds[7], (TOKENS, TOP), ((0, 4),), -0.2, 0.2), 0.1, 0.9)
    expert_ids_keys = jax.random.split(jax.random.fold_in(seeds[8], 1), TOKENS // TOK_DEV)
    expert_ids_turns = jax.random.permutation(jax.random.fold_in(seeds[8], 3), TOKENS // TOK_DEV)
    expert_ids = jax.vmap(lambda own, number: shared_out(jax.random.fold_in(seeds[8], 2), own, number, TOK_DEV, EXPERTS, TOP, CAP_E, 2))(expert_ids_keys, expert_ids_turns).reshape((TOKENS, TOP))
    expert_out = bell_draw(seeds[9], (GROUPS, 2 * EXPERTS * CAP, D), 0.0128, 0.079589844, ((0, 4), (1, 8)))
    return {"queries": queries, "key_rows": key_rows, "value_rows": value_rows, "out_grad": out_grad, "attn_out": attn_out, "doc_ids": doc_ids, "row_grad": row_grad, "gate_weights": gate_weights, "expert_ids": expert_ids, "expert_out": expert_out}


def slot_table(routes_block, experts_total, capacity):
    flat_ids = routes_block.reshape(-1).astype(jnp.int32)
    onehot = (flat_ids[:, None] == jnp.arange(experts_total, dtype=jnp.int32)[None, :]).astype(jnp.int32)
    earlier = jnp.cumsum(onehot, axis=0) - onehot
    ranking = lax.optimization_barrier(jnp.sum(earlier * onehot, axis=1))
    return (2 * flat_ids + ranking // capacity) * capacity + ranking % capacity

def route_group(packed):
    row_block, gate_block, route_block, stored = packed
    slot_count = 2 * EXPERTS * CAP
    positions = slot_table(route_block, EXPERTS, CAP)
    chosen = jnp.arange(slot_count, dtype=jnp.int32)[:, None] == positions[None, :]
    by_token = lax.optimization_barrier(jnp.sum(chosen.reshape(slot_count, TOK_DEV, TOP).astype(jnp.int32), axis=2))
    routed = jnp.dot(by_token.astype(jnp.bfloat16), row_block, preferred_element_type=jnp.float32).astype(jnp.bfloat16)
    slot_gates = lax.optimization_barrier(jnp.sum(jnp.where(chosen, gate_block.reshape(-1)[None, :], 0.0), axis=1))
    gate_part = lax.optimization_barrier(jnp.sum(routed.astype(jnp.float32) * stored.astype(jnp.float32), axis=1))
    expert_part = (slot_gates[:, None] * routed.astype(jnp.float32)).astype(jnp.bfloat16)
    return (gate_part, expert_part)

def reference(queries, key_rows, value_rows, out_grad, attn_out, doc_ids, row_grad, gate_weights, expert_ids, expert_out):
    scaling = 1.0 / math.sqrt(HD)
    positions = jnp.arange(TOKENS, dtype=jnp.int32)
    allowed = (doc_ids[:, None] == doc_ids[None, :]) & (positions[None, :] <= positions[:, None])
    group_size = H // KVH

    def one_head(head_index):
        group_index = head_index // group_size
        query_head = lax.dynamic_slice_in_dim(queries, head_index * HD, HD, 1)
        key_head = lax.dynamic_slice_in_dim(key_rows, group_index * HD, HD, 1)
        value_head = lax.dynamic_slice_in_dim(value_rows, group_index * HD, HD, 1)
        grad_head = lax.dynamic_slice_in_dim(out_grad, head_index * HD, HD, 1)
        output_head = lax.dynamic_slice_in_dim(attn_out, head_index * HD, HD, 1)
        scores = jnp.dot(query_head, key_head.T, preferred_element_type=jnp.float32) * scaling
        scores = jnp.where(allowed, scores, -1e+30)
        row_max = lax.optimization_barrier(jnp.max(scores, axis=1, keepdims=True))
        totals = lax.optimization_barrier(jnp.sum(jnp.where(allowed, jnp.exp(scores - row_max), 0.0), axis=1, keepdims=True))
        log_total = row_max + jnp.log(totals)
        probs = jnp.where(allowed, jnp.exp(scores - log_total), 0.0)
        probs_low = probs.astype(jnp.bfloat16)
        row_delta = lax.optimization_barrier(jnp.sum(grad_head.astype(jnp.float32) * output_head.astype(jnp.float32), axis=1, keepdims=True))
        prob_grad = jnp.dot(grad_head, value_head.T, preferred_element_type=jnp.float32)
        score_grad = (probs * (prob_grad - row_delta)).astype(jnp.bfloat16)
        query_part = (jnp.dot(score_grad, key_head, preferred_element_type=jnp.float32) * scaling).astype(jnp.bfloat16)
        key_part = jnp.dot(score_grad.T, query_head, preferred_element_type=jnp.float32) * scaling
        value_part = jnp.dot(probs_low.T, grad_head, preferred_element_type=jnp.float32)
        return (query_part, key_part, value_part)
    query_parts, key_parts, value_parts = lax.map(one_head, jnp.arange(H, dtype=jnp.int32))
    query_grad = jnp.transpose(query_parts, (1, 0, 2)).reshape(TOKENS, H * HD)
    key_sum = lax.optimization_barrier(jnp.sum(key_parts.reshape(KVH, group_size, TOKENS, HD), axis=1))
    value_sum = lax.optimization_barrier(jnp.sum(value_parts.reshape(KVH, group_size, TOKENS, HD), axis=1))
    key_grad = jnp.transpose(key_sum, (1, 0, 2)).reshape(TOKENS, KVH * HD).astype(jnp.bfloat16)
    value_grad = jnp.transpose(value_sum, (1, 0, 2)).reshape(TOKENS, KVH * HD).astype(jnp.bfloat16)
    gate_grad, expert_grad = lax.map(route_group, (row_grad.reshape(GROUPS, TOK_DEV, D), gate_weights.reshape(GROUPS, TOK_DEV, TOP), expert_ids.reshape(GROUPS, TOK_DEV, TOP), expert_out))
    return (query_grad, key_grad, value_grad, gate_grad, expert_grad)
```

```python
import functools
import math

import jax
import jax.numpy as jnp
from jax import lax
from jax.experimental import pallas as pl
from jax.experimental.pallas import tpu as pltpu
from jax.sharding import PartitionSpec as P

HD = 128
QH_DEV = 3
F32 = jnp.float32
BF16 = jnp.bfloat16
MESH = pl.DeviceIdType.MESH


def dot(a, b, dims):
    return lax.dot_general(a, b, (dims, ((), ())), preferred_element_type=F32)


def each(count, body):
    if count <= 4:
        for i in range(count):
            body(i)
    else:
        lax.fori_loop(0, count, lambda i, _: (body(i), 0)[1], 0)


def kernel(
    ctx_size,
    tp_size,
    reach,
    chunks,
    q_in,
    k_in,
    v_in,
    do_in,
    o_in,
    docs_in,
    rows_in,
    gates_in,
    ids_in,
    eo_in,
    dq_out,
    dk_out,
    dv_out,
    dgate_out,
    dexp_out,
    q_raw,
    do_raw,
    o_raw,
    docs,
    gates,
    ids,
    eo,
    kv,
    q_s,
    q_half,
    do_s,
    do_half,
    delta,
    score,
    score_max,
    score_sum,
    dq_acc,
    part_send,
    part_own,
    part_recv,
    rows,
    pick,
    slot_gate,
    y_send,
    y_recv,
    gate_acc,
    in_sem,
    rows_in_sem,
    kv_send_sem,
    kv_recv_sem,
    part_send_sem,
    part_recv_sem,
    row_send_sem,
    row_recv_sem,
    y_send_sem,
    y_recv_sem,
):
    c = lax.axis_index("ctx")
    t = lax.axis_index("tp")
    e, y = t // 2, t % 2
    partner = e * 2 + 1 - y
    experts = tp_size // 2
    n = q_in.shape[0]
    cap = eo.shape[0]
    width = rows_in.shape[1]
    piece = width // chunks
    scaling = 1.0 / math.sqrt(HD)
    head_cols = pl.ds(pl.multiple_of(e * HD, HD), HD)

    row_loads = [
        pltpu.make_async_copy(
            rows_in.at[:, pl.ds(k * piece, piece)], rows.at[e, k], rows_in_sem.at[k]
        )
        for k in range(chunks)
    ]
    loads = {
        name: pltpu.make_async_copy(src, dst, in_sem.at[i])
        for i, (name, src, dst) in enumerate(
            (
                ("k", k_in.at[:, head_cols], kv.at[0, 0]),
                ("v", v_in.at[:, head_cols], kv.at[0, 1]),
                ("ids", ids_in, ids),
                ("gates", gates_in, gates),
                ("q", q_in, q_raw),
                ("do", do_in, do_raw),
                ("o", o_in, o_raw),
                ("docs", docs_in, docs),
                ("eo", eo_in.at[0], eo),
            )
        )
    }
    for load in row_loads:
        load.start()
    for load in loads.values():
        load.start()

    barrier = pltpu.get_barrier_semaphore()

    def greet(ctx, tp):
        pl.semaphore_signal(barrier, inc=1, device_id=(ctx, tp), device_id_type=MESH)

    greet(c, partner)

    @pl.when(e > 0)
    def _():
        greet(c, t - 2)

    @pl.when(e < experts - 1)
    def _():
        greet(c, t + 2)

    greeted = 1 + (e > 0).astype(jnp.int32) + (e < experts - 1).astype(jnp.int32)
    for o in range(1, reach + 1):

        @pl.when(c >= o)
        def _():
            greet(c - o, t)
            greet(c - o, partner)

        @pl.when(c + o < ctx_size)
        def _():
            greet(c + o, t)
            greet(c + o, partner)

        greeted += 2 * (c >= o).astype(jnp.int32) + 2 * (c + o < ctx_size).astype(jnp.int32)
    pl.semaphore_wait(barrier, greeted)

    def row_copy(way, src_e, k):
        to = t + 2 if way == 0 else t - 2
        return pltpu.make_async_remote_copy(
            src_ref=rows.at[src_e, k],
            dst_ref=rows.at[src_e, k],
            send_sem=row_send_sem.at[way, src_e, k],
            recv_sem=row_recv_sem.at[src_e, k],
            device_id=(c, to),
            device_id_type=MESH,
        )

    def y_copy(src_e, k):
        return pltpu.make_async_remote_copy(
            src_ref=y_send.at[src_e, k],
            dst_ref=y_recv.at[src_e, k],
            send_sem=y_send_sem.at[src_e, k],
            recv_sem=y_recv_sem.at[src_e, k],
            device_id=(c, partner),
            device_id_type=MESH,
        )

    def kv_copy(o):
        return pltpu.make_async_remote_copy(
            src_ref=kv.at[0],
            dst_ref=kv.at[o],
            send_sem=kv_send_sem.at[o],
            recv_sem=kv_recv_sem.at[o],
            device_id=(c + o, t),
            device_id_type=MESH,
        )

    def part_copy(o, which):
        return pltpu.make_async_remote_copy(
            src_ref=part_send.at[o, which],
            dst_ref=part_recv.at[o, which],
            send_sem=part_send_sem.at[o, which],
            recv_sem=part_recv_sem.at[o, which],
            device_id=(c - o, t if which == 0 else partner),
            device_id_type=MESH,
        )

    for k in range(chunks):
        row_loads[k].wait()

        @pl.when(e < experts - 1)
        def _():
            row_copy(0, e, k).start()

        @pl.when(e > 0)
        def _():
            row_copy(1, e, k).start()

    loads["k"].wait()
    loads["v"].wait()
    for o in range(1, reach + 1):

        @pl.when(c + o < ctx_size)
        def _():
            kv_copy(o).start()

    loads["ids"].wait()
    loads["gates"].wait()
    named = ids[...] == e
    hit = jnp.sum(jnp.where(named, 1.0, 0.0), axis=1, keepdims=True)
    gate = jnp.sum(jnp.where(named, gates[...], 0.0), axis=1, keepdims=True)
    row_i = lax.broadcasted_iota(jnp.int32, (n, n), 0)
    col_i = lax.broadcasted_iota(jnp.int32, (n, n), 1)
    before = jnp.where(col_i < row_i, 1.0, 0.0).astype(BF16)
    rank = dot(before, jnp.broadcast_to(hit, (n, 2 * cap)).astype(BF16), ((1,), (0,)))
    slot = lax.broadcasted_iota(jnp.int32, (n, 2 * cap), 1)
    slot = jnp.where(slot < cap, slot + cap * y, slot - cap * y).astype(F32)
    chosen = jnp.where(rank == slot, hit, 0.0)
    pick[...] = chosen.T.astype(BF16)
    slot_gate[...] = jnp.sum((chosen * gate).T, axis=1, keepdims=True)[:cap]
    gate_acc[...] = jnp.zeros_like(gate_acc)

    def finish(src, k, routed):
        cols = pl.ds(pl.multiple_of(src * width + k * piece, HD), piece)
        product = routed * eo[:, cols].astype(F32)
        total = gate_acc[...]
        for i in range(piece // HD):
            total += product[:, i * HD : (i + 1) * HD]
        gate_acc[...] = total
        dexp_out[0, :, cols] = (slot_gate[...] * routed).astype(BF16)

    def take(src_e, k):
        picked = dot(pick[...], rows[src_e, k], ((1,), (0,)))
        y_send[src_e, k] = picked[cap:].astype(BF16)
        y_copy(src_e, k).start()
        finish(src_e * 2 + y, k, picked[:cap])

    def take_other(src_e, k):
        y_copy(src_e, k).wait_recv()
        finish(src_e * 2 + 1 - y, k, y_recv[src_e, k].astype(F32))

    loads["eo"].wait()
    for k in range(chunks):
        take(e, k)

    loads["q"].wait()
    loads["do"].wait()
    loads["o"].wait()
    loads["docs"].wait()
    for h in range(QH_DEV):
        at, cols = slice(h * n, (h + 1) * n), slice(h * HD, (h + 1) * HD)
        query, grad, output = q_raw[:, cols], do_raw[:, cols], o_raw[:, cols]
        q_s[at] = query
        do_s[at] = grad
        query, grad = query.astype(F32), grad.astype(F32)
        delta[at] = jnp.sum(grad * output.astype(F32), axis=1, keepdims=True)
        q_half[at] = jnp.where(y == 0, query, pltpu.roll(query, HD // 2, 1)).astype(BF16)
        do_half[at] = jnp.where(y == 1, grad, pltpu.roll(grad, HD // 2, 1)).astype(BF16)

    q_docs = jnp.broadcast_to(docs[pl.ds(c, 1), :].astype(F32), (n, n)).T
    score_max[...] = jnp.full_like(score_max, -1e30)
    score_sum[...] = jnp.zeros_like(score_sum)
    dq_acc[...] = jnp.zeros_like(dq_acc)

    def scores_of(o):
        present = c >= o

        @pl.when(jnp.logical_and(o > 0, present))
        def _():
            kv_copy(o).wait_recv()

        @pl.when(jnp.logical_not(present))
        def _():
            kv[o] = jnp.zeros(kv.shape[1:], BF16)

        k_docs = docs[pl.ds(jnp.maximum(c - o, 0), 1), :].astype(F32)
        allowed = (k_docs == q_docs) & (col_i - o * n <= row_i) & present
        s = dot(q_s[...], kv[o, 0], ((1,), (1,))) * scaling
        s = jnp.where(jnp.concatenate([allowed] * QH_DEV, axis=0), s, -1e30)
        score[o] = s
        score_max[...] = jnp.maximum(score_max[...], s)

    each(reach + 1, scores_of)
    row_max = jnp.max(score_max[...], axis=1, keepdims=True)
    score_max[...] = jnp.broadcast_to(row_max, score_max.shape)

    def exp_of(o):
        p = jnp.exp(score[o] - score_max[...])
        score[o] = p
        score_sum[...] += p

    each(reach + 1, exp_of)
    inverse = 1.0 / jnp.sum(score_sum[...], axis=1, keepdims=True)
    score_sum[...] = jnp.broadcast_to(inverse, score_sum.shape)
    low = lax.broadcasted_iota(jnp.int32, (n, HD), 1) < HD // 2

    def grads_of(i):
        o = reach - i
        probs = score[o] * score_sum[...]
        prob_grad = dot(do_s[...], kv[o, 1], ((1,), (1,)))
        score_grad = (probs * (prob_grad - delta[...])).astype(BF16)
        dq_acc[...] += dot(score_grad, kv[o, 0], ((1,), (0,)))
        dk = dot(score_grad, q_half[...], ((0,), (0,))) * scaling
        dv = dot(probs.astype(BF16), do_half[...], ((0,), (0,)))
        own, other = jnp.where(low, dk, dv), jnp.where(low, dv, dk)
        part_send[o, 1] = other.astype(BF16)

        @pl.when(o == 0)
        def _():
            part_own[...] = own

        @pl.when(jnp.logical_and(o > 0, c >= o))
        def _():
            part_send[o, 0] = own.astype(BF16)
            part_copy(o, 0).start()

        @pl.when(c >= o)
        def _():
            part_copy(o, 1).start()

    each(reach + 1, grads_of)
    for h in range(QH_DEV):
        dq_out[:, h * HD : (h + 1) * HD] = (dq_acc[h * n : (h + 1) * n] * scaling).astype(BF16)

    def sources(step):
        return ((0, e - step, e >= step), (1, e + step, e + step < experts))

    def arrive(step):
        for k in range(chunks):
            for way, src_e, present in sources(step):

                @pl.when(present)
                def _():
                    row_copy(way, src_e, k).wait_recv()

                    @pl.when(e < experts - 1 if way == 0 else e > 0)
                    def _():
                        row_copy(way, src_e, k).start()

                    take(src_e, k)

    def arrive_other(step):
        for k in range(chunks):
            if step == 0:
                take_other(e, k)
                continue
            for _way, src_e, present in sources(step):

                @pl.when(present)
                def _():
                    take_other(src_e, k)

    def sum_parts():
        kept, other = part_own[...], None
        part_copy(0, 1).wait_recv()
        part_own[...] = kept + pltpu.roll(part_recv[0, 1].astype(F32), HD // 2, 1)
        for o in range(1, reach + 1):

            @pl.when(c + o < ctx_size)
            def _():
                part_copy(o, 0).wait_recv()
                part_copy(o, 1).wait_recv()
                part_own[...] += part_recv[o, 0].astype(F32) + pltpu.roll(
                    part_recv[o, 1].astype(F32), HD // 2, 1
                )

        summed = part_own[...].astype(BF16)
        dk_out[...] = summed[:, : HD // 2]
        dv_out[...] = summed[:, HD // 2 :]

    for step in range(1, experts):
        arrive(step)
        arrive_other(step - 1)
        if step == max(1, experts - 2):
            sum_parts()
    arrive_other(experts - 1)

    gate_sum = jnp.sum(gate_acc[...], axis=1, keepdims=True)
    dgate_out[...] = jnp.broadcast_to(gate_sum, (cap, HD)).T[:1]

    for k in range(chunks):

        @pl.when(e < experts - 1)
        def _():
            row_copy(0, e, k).wait_send()

        @pl.when(e > 0)
        def _():
            row_copy(1, e, k).wait_send()

        y_copy(e, k).wait_send()
        for step in range(1, experts):
            for way, src_e, present in sources(step):

                @pl.when(present)
                def _():
                    y_copy(src_e, k).wait_send()

                    @pl.when(e < experts - 1 if way == 0 else e > 0)
                    def _():
                        row_copy(way, src_e, k).wait_send()

    part_copy(0, 1).wait_send()
    for o in range(1, reach + 1):

        @pl.when(c + o < ctx_size)
        def _():
            kv_copy(o).wait_send()

        @pl.when(c >= o)
        def _():
            part_copy(o, 0).wait_send()
            part_copy(o, 1).wait_send()


def local(
    queries,
    key_rows,
    value_rows,
    out_grad,
    attn_out,
    doc_ids,
    row_grad,
    gate_weights,
    expert_ids,
    expert_out,
):
    ctx_size, tp_size = lax.axis_size("ctx"), lax.axis_size("tp")
    n, width = row_grad.shape
    cap, features = expert_out.shape[1:]
    experts = tp_size // 2
    reach = min((doc_ids.shape[0] // 2 + n) // n, ctx_size - 1)
    chunks = 3 if width % (3 * HD) == 0 else 1
    piece = width // chunks
    blocks = reach + 1
    stacked = QH_DEV * n
    dma = pltpu.SemaphoreType.DMA
    return pl.pallas_call(
        functools.partial(kernel, ctx_size, tp_size, reach, chunks),
        out_shape=(
            jax.ShapeDtypeStruct(queries.shape, BF16),
            jax.ShapeDtypeStruct((n, HD // 2), BF16),
            jax.ShapeDtypeStruct((n, HD // 2), BF16),
            jax.ShapeDtypeStruct((1, cap), F32),
            jax.ShapeDtypeStruct(expert_out.shape, BF16),
        ),
        in_specs=[pl.BlockSpec(memory_space=pl.ANY)] * 10,
        out_specs=[pl.BlockSpec(memory_space=pltpu.VMEM)] * 5,
        scratch_shapes=[
            pltpu.VMEM(queries.shape, BF16),
            pltpu.VMEM(queries.shape, BF16),
            pltpu.VMEM(queries.shape, BF16),
            pltpu.VMEM((doc_ids.shape[0] // n, n), jnp.int32),
            pltpu.VMEM(gate_weights.shape, F32),
            pltpu.VMEM(expert_ids.shape, jnp.int32),
            pltpu.VMEM((cap, features), BF16),
            pltpu.VMEM((blocks, 2, n, HD), BF16),
            pltpu.VMEM((stacked, HD), BF16),
            pltpu.VMEM((stacked, HD), BF16),
            pltpu.VMEM((stacked, HD), BF16),
            pltpu.VMEM((stacked, HD), BF16),
            pltpu.VMEM((stacked, 1), F32),
            pltpu.VMEM((blocks, stacked, n), F32),
            pltpu.VMEM((stacked, n), F32),
            pltpu.VMEM((stacked, n), F32),
            pltpu.VMEM((stacked, HD), F32),
            pltpu.VMEM((blocks, 2, n, HD), BF16),
            pltpu.VMEM((n, HD), F32),
            pltpu.VMEM((blocks, 2, n, HD), BF16),
            pltpu.VMEM((experts, chunks, n, piece), BF16),
            pltpu.VMEM((2 * cap, n), BF16),
            pltpu.VMEM((cap, 1), F32),
            pltpu.VMEM((experts, chunks, cap, piece), BF16),
            pltpu.VMEM((experts, chunks, cap, piece), BF16),
            pltpu.VMEM((cap, HD), F32),
            dma((9,)),
            dma((chunks,)),
            dma((blocks,)),
            dma((blocks,)),
            dma((blocks, 2)),
            dma((blocks, 2)),
            dma((2, experts, chunks)),
            dma((experts, chunks)),
            dma((experts, chunks)),
            dma((experts, chunks)),
        ],
        compiler_params=pltpu.CompilerParams(
            collective_id=0, has_side_effects=True, vmem_limit_bytes=40 * 1024 * 1024
        ),
        name="backward",
    )(
        queries,
        key_rows,
        value_rows,
        out_grad,
        attn_out,
        doc_ids.reshape(-1, n),
        row_grad,
        gate_weights,
        expert_ids,
        expert_out,
    )


def solution(mesh):
    in_specs = (
        P("ctx", "tp"),
        P("ctx", None),
        P("ctx", None),
        P("ctx", "tp"),
        P("ctx", "tp"),
        P(),
        P("ctx", "tp"),
        P("ctx", None),
        P("ctx", None),
        P("ctx", "tp", None),
    )
    out_specs = (
        P("ctx", "tp"),
        P("ctx", "tp"),
        P("ctx", "tp"),
        P("ctx", "tp"),
        P("ctx", "tp", None),
    )
    return jax.shard_map(local, mesh=mesh, in_specs=in_specs, out_specs=out_specs, check_vma=False)
```

```python
import functools
import math

import jax
import jax.numpy as jnp
from jax import lax
from jax.experimental import pallas as pl
from jax.experimental.pallas import tpu as pltpu
from jax.sharding import PartitionSpec as P

HD = 128
QH_DEV = 3
F32 = jnp.float32
BF16 = jnp.bfloat16
MESH = pl.DeviceIdType.MESH
VMEM = 62 * 1024 * 1024


def dot(a, b, dims):
    return lax.dot_general(a, b, (dims, ((), ())), preferred_element_type=F32)


def each(count, body):
    if count <= 4:
        for i in range(count):
            body(i)
    else:
        lax.fori_loop(0, count, lambda i, _: (body(i), 0)[1], 0)


def kernel(
    ctx_size,
    tp_size,
    reach,
    chunks,
    q_in,
    k_in,
    v_in,
    do_in,
    o_in,
    docs_in,
    rows_in,
    gates_in,
    ids_in,
    eo_in,
    dq_hbm,
    dk_hbm,
    dv_hbm,
    dgate_hbm,
    dexp_hbm,
    dq_out,
    dk_out,
    dv_out,
    dgate_out,
    dexp_out,
    q_raw,
    do_raw,
    o_raw,
    docs,
    gates,
    ids,
    eo,
    kv,
    q_s,
    q_half,
    do_s,
    do_half,
    delta,
    score,
    score_max,
    score_sum,
    dq_acc,
    part_send,
    part_own,
    part_recv,
    rows,
    pick,
    slot_gate,
    y_send,
    y_recv,
    gate_acc,
    in_sem,
    rows_in_sem,
    kv_send_sem,
    kv_recv_sem,
    part_send_sem,
    part_recv_sem,
    row_send_sem,
    row_recv_sem,
    y_send_sem,
    y_recv_sem,
    out_sem,
    dexp_sem,
):
    c = lax.axis_index("ctx")
    t = lax.axis_index("tp")
    e, y = t // 2, t % 2
    partner = e * 2 + 1 - y
    experts = tp_size // 2
    n = q_in.shape[0]
    cap = eo.shape[0]
    width = rows_in.shape[1]
    piece = width // chunks
    scaling = 1.0 / math.sqrt(HD)
    head_cols = pl.ds(pl.multiple_of(e * HD, HD), HD)

    row_loads = [
        pltpu.make_async_copy(
            rows_in.at[:, pl.ds(k * piece, piece)], rows.at[e, k], rows_in_sem.at[k]
        )
        for k in range(chunks)
    ]
    loads = {
        name: pltpu.make_async_copy(src, dst, in_sem.at[i])
        for i, (name, src, dst) in enumerate(
            (
                ("k", k_in.at[:, head_cols], kv.at[0, 0]),
                ("v", v_in.at[:, head_cols], kv.at[0, 1]),
                ("ids", ids_in, ids),
                ("gates", gates_in, gates),
                ("q", q_in, q_raw),
                ("do", do_in, do_raw),
                ("o", o_in, o_raw),
                ("docs", docs_in, docs),
                ("eo", eo_in.at[0], eo),
            )
        )
    }
    for load in row_loads:
        load.start()
    for load in loads.values():
        load.start()

    barrier = pltpu.get_barrier_semaphore()

    def greet(ctx, tp):
        pl.semaphore_signal(barrier, inc=1, device_id=(ctx, tp), device_id_type=MESH)

    greet(c, partner)

    @pl.when(e > 0)
    def _():
        greet(c, t - 2)

    @pl.when(e < experts - 1)
    def _():
        greet(c, t + 2)

    greeted = 1 + (e > 0).astype(jnp.int32) + (e < experts - 1).astype(jnp.int32)
    for o in range(1, reach + 1):

        @pl.when(c >= o)
        def _():
            greet(c - o, t)
            greet(c - o, partner)

        @pl.when(c + o < ctx_size)
        def _():
            greet(c + o, t)
            greet(c + o, partner)

        greeted += 2 * (c >= o).astype(jnp.int32) + 2 * (c + o < ctx_size).astype(jnp.int32)
    pl.semaphore_wait(barrier, greeted)

    def row_copy(way, src_e, k):
        to = t + 2 if way == 0 else t - 2
        return pltpu.make_async_remote_copy(
            src_ref=rows.at[src_e, k],
            dst_ref=rows.at[src_e, k],
            send_sem=row_send_sem.at[way, src_e, k],
            recv_sem=row_recv_sem.at[src_e, k],
            device_id=(c, to),
            device_id_type=MESH,
        )

    def y_copy(src_e, k):
        return pltpu.make_async_remote_copy(
            src_ref=y_send.at[src_e, k],
            dst_ref=y_recv.at[src_e, k],
            send_sem=y_send_sem.at[src_e, k],
            recv_sem=y_recv_sem.at[src_e, k],
            device_id=(c, partner),
            device_id_type=MESH,
        )

    def kv_copy(o):
        return pltpu.make_async_remote_copy(
            src_ref=kv.at[0],
            dst_ref=kv.at[o],
            send_sem=kv_send_sem.at[o],
            recv_sem=kv_recv_sem.at[o],
            device_id=(c + o, t),
            device_id_type=MESH,
        )

    def part_copy(o, which):
        return pltpu.make_async_remote_copy(
            src_ref=part_send.at[o, which],
            dst_ref=part_recv.at[o, which],
            send_sem=part_send_sem.at[o, which],
            recv_sem=part_recv_sem.at[o, which],
            device_id=(c - o, t if which == 0 else partner),
            device_id_type=MESH,
        )

    for k in range(chunks):
        row_loads[k].wait()

        @pl.when(e < experts - 1)
        def _():
            row_copy(0, e, k).start()

        @pl.when(e > 0)
        def _():
            row_copy(1, e, k).start()

    loads["k"].wait()
    loads["v"].wait()
    for o in range(1, reach + 1):

        @pl.when(c + o < ctx_size)
        def _():
            kv_copy(o).start()

    loads["ids"].wait()
    loads["gates"].wait()
    named = ids[...] == e
    hit = jnp.sum(jnp.where(named, 1.0, 0.0), axis=0, keepdims=True)
    gate = jnp.sum(jnp.where(named, gates[...], 0.0), axis=0, keepdims=True)
    hit = jnp.broadcast_to(hit, (2 * cap, n)).T
    row_i = lax.broadcasted_iota(jnp.int32, (n, n), 0)
    col_i = lax.broadcasted_iota(jnp.int32, (n, n), 1)
    before = jnp.where(col_i < row_i, 1.0, 0.0).astype(BF16)
    rank = dot(before, hit.astype(BF16), ((1,), (0,)))
    slot = lax.broadcasted_iota(jnp.int32, (n, 2 * cap), 1)
    slot = jnp.where(slot < cap, slot + cap * y, slot - cap * y).astype(F32)
    chosen = jnp.where(rank == slot, hit, 0.0)
    chosen = chosen.T
    pick[...] = chosen.astype(BF16)
    slot_gate[...] = jnp.sum(chosen * gate, axis=1, keepdims=True)[:cap]
    gate_acc[...] = jnp.zeros_like(gate_acc)

    def dexp_copy(src, k):
        cols = pl.ds(pl.multiple_of(src * width + k * piece, HD), piece)
        return pltpu.make_async_copy(
            dexp_out.at[:, cols], dexp_hbm.at[0, :, cols], dexp_sem.at[src, k]
        )

    out_copies = [
        pltpu.make_async_copy(source, target, out_sem.at[i])
        for i, (source, target) in enumerate(
            ((dq_out, dq_hbm), (dk_out, dk_hbm), (dv_out, dv_hbm), (dgate_out, dgate_hbm))
        )
    ]

    def finish(src, k, routed):
        cols = pl.ds(pl.multiple_of(src * width + k * piece, HD), piece)
        product = routed * eo[:, cols].astype(F32)
        total = gate_acc[...]
        for i in range(piece // HD):
            total += product[:, i * HD : (i + 1) * HD]
        gate_acc[...] = total
        dexp_out[:, cols] = (slot_gate[...] * routed).astype(BF16)
        dexp_copy(src, k).start()

    def take(src_e, k):
        picked = dot(pick[...], rows[src_e, k], ((1,), (0,)))
        y_send[src_e, k] = picked[cap:].astype(BF16)
        y_copy(src_e, k).start()
        finish(src_e * 2 + y, k, picked[:cap])

    def take_other(src_e, k):
        y_copy(src_e, k).wait_recv()
        finish(src_e * 2 + 1 - y, k, y_recv[src_e, k].astype(F32))

    loads["eo"].wait()
    for k in range(chunks):
        take(e, k)

    loads["q"].wait()
    loads["do"].wait()
    loads["o"].wait()
    loads["docs"].wait()
    for h in range(QH_DEV):
        at, cols = slice(h * n, (h + 1) * n), slice(h * HD, (h + 1) * HD)
        query, grad, output = q_raw[:, cols], do_raw[:, cols], o_raw[:, cols]
        q_s[at] = query
        do_s[at] = grad
        query, grad = query.astype(F32), grad.astype(F32)
        delta[at] = jnp.sum(grad * output.astype(F32), axis=1, keepdims=True)
        q_half[at] = jnp.where(y == 0, query, pltpu.roll(query, HD // 2, 1)).astype(BF16)
        do_half[at] = jnp.where(y == 1, grad, pltpu.roll(grad, HD // 2, 1)).astype(BF16)

    q_docs = jnp.broadcast_to(docs[pl.ds(c, 1), :].astype(F32), (n, n)).T
    score_max[...] = jnp.full_like(score_max, -1e30)
    score_sum[...] = jnp.zeros_like(score_sum)
    dq_acc[...] = jnp.zeros_like(dq_acc)

    def scores_of(o):
        k_docs = docs[pl.ds(jnp.maximum(c - o, 0), 1), :].astype(F32)
        allowed = (k_docs == q_docs) & (col_i - o * n <= row_i) & (c >= o)
        s = dot(q_s[...], kv[o, 0], ((1,), (1,))) * scaling
        s = jnp.where(jnp.concatenate([allowed] * QH_DEV, axis=0), s, -1e30)
        score[o] = s
        score_max[...] = jnp.maximum(score_max[...], s)

    for o in range(1, reach + 1):

        @pl.when(c >= o)
        def _():
            kv_copy(o).wait_recv()

        @pl.when(c < o)
        def _():
            kv[o] = jnp.zeros(kv.shape[1:], BF16)

    each(reach + 1, scores_of)
    row_max = jnp.max(score_max[...], axis=1, keepdims=True)
    score_max[...] = jnp.broadcast_to(row_max, score_max.shape)

    def exp_of(o):
        p = jnp.exp(score[o] - score_max[...])
        score[o] = p
        score_sum[...] += p

    each(reach + 1, exp_of)
    inverse = 1.0 / jnp.sum(score_sum[...], axis=1, keepdims=True)
    score_sum[...] = jnp.broadcast_to(inverse, score_sum.shape)
    low = lax.broadcasted_iota(jnp.int32, (n, HD), 1) < HD // 2

    def grads_of(o):
        probs = score[o] * score_sum[...]
        prob_grad = dot(do_s[...], kv[o, 1], ((1,), (1,)))
        score_grad = (probs * (prob_grad - delta[...])).astype(BF16)
        dq_acc[...] += dot(score_grad, kv[o, 0], ((1,), (0,)))
        dk = dot(score_grad, q_half[...], ((0,), (0,))) * scaling
        dv = dot(probs.astype(BF16), do_half[...], ((0,), (0,)))
        own = jnp.where(low, dk, dv)
        part_send[o, 1] = jnp.where(low, dv, dk).astype(BF16)
        if isinstance(o, int) and o == 0:
            part_own[...] = own
        else:
            part_send[o, 0] = own.astype(BF16)

    def send_parts(o):
        @pl.when(c >= o)
        def _():
            part_copy(o, 0).start()
            part_copy(o, 1).start()

    def forward(step, k):
        for way, src_e, present in sources(step):

            @pl.when(present)
            def _():
                row_copy(way, src_e, k).wait_recv()

                @pl.when(e < experts - 1 if way == 0 else e > 0)
                def _():
                    row_copy(way, src_e, k).start()

    def sources(step):
        return ((0, e - step, e >= step), (1, e + step, e + step < experts))

    early = 0
    if reach <= 3:
        while early < chunks - 1:
            forward(1, early)
            early += 1
        late = list(range(reach, reach // 2, -1))
        for o in late:
            grads_of(o)
        for o in late:
            send_parts(o)
        while early < chunks:
            forward(1, early)
            early += 1
        near = list(range(reach // 2, -1, -1))
        for o in near:
            grads_of(o)
        for o in near[:-1]:
            send_parts(o)
    else:

        @pl.loop(0, reach)
        def _(i):
            grads_of(reach - i)
            send_parts(reach - i)

        grads_of(0)
    part_copy(0, 1).start()
    for h in range(QH_DEV):
        dq_out[:, h * HD : (h + 1) * HD] = (dq_acc[h * n : (h + 1) * n] * scaling).astype(BF16)
    out_copies[0].start()

    def arrive(step):
        for k in range(chunks):
            if step > 1 or k >= early:
                forward(step, k)
            for _way, src_e, present in sources(step):

                @pl.when(present)
                def _():
                    take(src_e, k)

    def arrive_other(step):
        for k in range(chunks):
            if step == 0:
                take_other(e, k)
                continue
            for _way, src_e, present in sources(step):

                @pl.when(present)
                def _():
                    take_other(src_e, k)

    def sum_parts():
        part_copy(0, 1).wait_recv()
        part_own[...] += pltpu.roll(part_recv[0, 1].astype(F32), HD // 2, 1)
        for o in range(1, reach + 1):

            @pl.when(c + o < ctx_size)
            def _():
                part_copy(o, 0).wait_recv()
                part_copy(o, 1).wait_recv()
                part_own[...] += part_recv[o, 0].astype(F32) + pltpu.roll(
                    part_recv[o, 1].astype(F32), HD // 2, 1
                )

        summed = part_own[...].T.astype(BF16)
        dk_out[...] = summed[: HD // 2]
        dv_out[...] = summed[HD // 2 :]
        out_copies[1].start()
        out_copies[2].start()

    for step in range(1, experts):
        arrive(step)
        arrive_other(step - 1)
        if step == max(1, experts - 2):
            sum_parts()
    arrive_other(experts - 1)

    gate_sum = jnp.sum(gate_acc[...], axis=1, keepdims=True)
    dgate_out[...] = jnp.broadcast_to(gate_sum, (cap, HD)).T[:1]
    out_copies[3].start()

    for k in range(chunks):

        @pl.when(e < experts - 1)
        def _():
            row_copy(0, e, k).wait_send()

        @pl.when(e > 0)
        def _():
            row_copy(1, e, k).wait_send()

        y_copy(e, k).wait_send()
        for step in range(1, experts):
            for way, src_e, present in sources(step):

                @pl.when(present)
                def _():
                    y_copy(src_e, k).wait_send()

                    @pl.when(e < experts - 1 if way == 0 else e > 0)
                    def _():
                        row_copy(way, src_e, k).wait_send()

    for copy in out_copies:
        copy.wait()
    for src in range(tp_size):
        for k in range(chunks):
            dexp_copy(src, k).wait()
    part_copy(0, 1).wait_send()
    for o in range(1, reach + 1):

        @pl.when(c + o < ctx_size)
        def _():
            kv_copy(o).wait_send()

        @pl.when(c >= o)
        def _():
            part_copy(o, 0).wait_send()
            part_copy(o, 1).wait_send()


def write(*refs):
    sources, targets, sem = list(refs[:5]), list(refs[5:10]), refs[10]
    large_in, large_out = sources.pop(), targets.pop()
    for row in range(0, large_in.shape[1], 16):
        sources.append(large_in.at[0, pl.ds(row, 16)])
        targets.append(large_out.at[0, pl.ds(row, 16)])
    copies = [
        pltpu.make_async_copy(source, target, sem.at[i])
        for i, (source, target) in enumerate(zip(sources, targets))
    ]
    for copy in reversed(copies):
        copy.start()
    for copy in copies:
        copy.wait()


def local(
    queries,
    key_rows,
    value_rows,
    out_grad,
    attn_out,
    doc_ids,
    row_grad,
    gate_weights,
    expert_ids,
    expert_out,
):
    ctx_size, tp_size = lax.axis_size("ctx"), lax.axis_size("tp")
    n, width = row_grad.shape
    cap, features = expert_out.shape[1:]
    experts = tp_size // 2
    reach = min((doc_ids.shape[0] // 2 + n) // n, ctx_size - 1)
    chunks = 3 if width % (3 * HD) == 0 else 1
    piece = width // chunks
    blocks = reach + 1
    stacked = QH_DEV * n
    dma = pltpu.SemaphoreType.DMA
    out_shape = (
        jax.ShapeDtypeStruct(queries.shape, BF16),
        jax.ShapeDtypeStruct((HD // 2, n), BF16),
        jax.ShapeDtypeStruct((HD // 2, n), BF16),
        jax.ShapeDtypeStruct((1, cap), F32),
        jax.ShapeDtypeStruct(expert_out.shape, BF16),
    )
    outs = pl.pallas_call(
        functools.partial(kernel, ctx_size, tp_size, reach, chunks),
        out_shape=out_shape,
        in_specs=[pl.BlockSpec(memory_space=pltpu.HBM)] * 10,
        out_specs=[pl.BlockSpec(memory_space=pltpu.HBM)] * 5,
        scratch_shapes=[
            *(pltpu.VMEM(out.shape, out.dtype) for out in out_shape[:4]),
            pltpu.VMEM((cap, features), BF16),
            pltpu.VMEM(queries.shape, BF16),
            pltpu.VMEM(queries.shape, BF16),
            pltpu.VMEM(queries.shape, BF16),
            pltpu.VMEM((doc_ids.shape[0] // n, n), jnp.int32),
            pltpu.VMEM(gate_weights.shape[::-1], F32),
            pltpu.VMEM(expert_ids.shape[::-1], jnp.int32),
            pltpu.VMEM((cap, features), BF16),
            pltpu.VMEM((blocks, 2, n, HD), BF16),
            pltpu.VMEM((stacked, HD), BF16),
            pltpu.VMEM((stacked, HD), BF16),
            pltpu.VMEM((stacked, HD), BF16),
            pltpu.VMEM((stacked, HD), BF16),
            pltpu.VMEM((stacked, 1), F32),
            pltpu.VMEM((blocks, stacked, n), F32),
            pltpu.VMEM((stacked, n), F32),
            pltpu.VMEM((stacked, n), F32),
            pltpu.VMEM((stacked, HD), F32),
            pltpu.VMEM((blocks, 2, n, HD), BF16),
            pltpu.VMEM((n, HD), F32),
            pltpu.VMEM((blocks, 2, n, HD), BF16),
            pltpu.VMEM((experts, chunks, n, piece), BF16),
            pltpu.VMEM((2 * cap, n), BF16),
            pltpu.VMEM((cap, 1), F32),
            pltpu.VMEM((experts, chunks, cap, piece), BF16),
            pltpu.VMEM((experts, chunks, cap, piece), BF16),
            pltpu.VMEM((cap, HD), F32),
            dma((9,)),
            dma((chunks,)),
            dma((blocks,)),
            dma((blocks,)),
            dma((blocks, 2)),
            dma((blocks, 2)),
            dma((2, experts, chunks)),
            dma((experts, chunks)),
            dma((experts, chunks)),
            dma((experts, chunks)),
            dma((4,)),
            dma((tp_size, chunks)),
        ],
        compiler_params=pltpu.CompilerParams(
            collective_id=0, has_side_effects=True, vmem_limit_bytes=VMEM
        ),
        name="backward",
    )(
        queries,
        key_rows,
        value_rows,
        out_grad,
        attn_out,
        doc_ids.reshape(-1, n),
        row_grad,
        gate_weights.T,
        expert_ids.T,
        expert_out,
    )
    query_grad, key_grad, value_grad, gate_grad, expert_grad = pl.pallas_call(
        write,
        out_shape=out_shape,
        in_specs=[pl.BlockSpec(memory_space=pltpu.HBM)] * 5,
        out_specs=[pl.BlockSpec(memory_space=pltpu.HBM)] * 5,
        scratch_shapes=[dma((4 + cap // 16,))],
        compiler_params=pltpu.CompilerParams(vmem_limit_bytes=VMEM),
        name="write",
    )(*outs)
    return (query_grad, key_grad.T, value_grad.T, gate_grad, expert_grad)


def solution(mesh):
    in_specs = (
        P("ctx", "tp"),
        P("ctx", None),
        P("ctx", None),
        P("ctx", "tp"),
        P("ctx", "tp"),
        P(),
        P("ctx", "tp"),
        P("ctx", None),
        P("ctx", None),
        P("ctx", "tp", None),
    )
    out_specs = (
        P("ctx", "tp"),
        P("ctx", "tp"),
        P("ctx", "tp"),
        P("ctx", "tp"),
        P("ctx", "tp", None),
    )
    return jax.shard_map(local, mesh=mesh, in_specs=in_specs, out_specs=out_specs, check_vma=False)
```

```python
import functools
import math

import jax
import jax.numpy as jnp
from jax import lax
from jax.experimental import pallas as pl
from jax.experimental.pallas import tpu as pltpu
from jax.sharding import PartitionSpec as P

HD = 128
QH_DEV = 3
F32 = jnp.float32
BF16 = jnp.bfloat16
MESH = pl.DeviceIdType.MESH
VMEM = 62 * 1024 * 1024


def dot(a, b, dims):
    return lax.dot_general(a, b, (dims, ((), ())), preferred_element_type=F32)


def each(count, body):
    if count <= 4:
        for i in range(count):
            body(i)
    else:
        lax.fori_loop(0, count, lambda i, _: (body(i), 0)[1], 0)


def kernel(
    ctx_size,
    tp_size,
    reach,
    chunks,
    q_in,
    k_in,
    v_in,
    do_in,
    o_in,
    docs_in,
    rows_in,
    gates_in,
    ids_in,
    eo_in,
    dq_hbm,
    dk_hbm,
    dv_hbm,
    dgate_hbm,
    dexp_hbm,
    dq_out,
    dk_out,
    dv_out,
    dgate_out,
    dexp_out,
    q_raw,
    do_raw,
    o_raw,
    docs,
    gates,
    ids,
    eo,
    kv,
    q_s,
    q_half,
    do_s,
    do_half,
    delta,
    score,
    score_max,
    score_sum,
    dq_acc,
    part_send,
    part_own,
    part_recv,
    rows,
    pick,
    slot_gate,
    y_send,
    y_recv,
    gate_acc,
    in_sem,
    rows_in_sem,
    kv_send_sem,
    kv_recv_sem,
    part_send_sem,
    part_recv_sem,
    row_send_sem,
    row_recv_sem,
    y_send_sem,
    y_recv_sem,
    out_sem,
    dexp_sem,
):
    c = lax.axis_index("ctx")
    t = lax.axis_index("tp")
    e, y = t // 2, t % 2
    partner = e * 2 + 1 - y
    experts = tp_size // 2
    n = q_in.shape[0]
    cap = eo.shape[0]
    width = rows_in.shape[1]
    piece = width // chunks
    scaling = 1.0 / math.sqrt(HD)
    head_cols = pl.ds(pl.multiple_of(e * HD, HD), HD)

    def cut(k):
        return pl.ds(k * piece, piece)

    row_loads = [
        pltpu.make_async_copy(
            rows_in.at[:, cut(k)], rows.at[e, :, cut(k)], rows_in_sem.at[k]
        )
        for k in range(chunks)
    ]
    loads = {
        name: pltpu.make_async_copy(src, dst, in_sem.at[i])
        for i, (name, src, dst) in enumerate(
            (
                ("k", k_in.at[:, head_cols], kv.at[0, 0]),
                ("v", v_in.at[:, head_cols], kv.at[0, 1]),
                ("ids", ids_in, ids),
                ("gates", gates_in, gates),
                ("q", q_in, q_raw),
                ("do", do_in, do_raw),
                ("o", o_in, o_raw),
                ("docs", docs_in, docs),
                ("eo", eo_in.at[0], eo),
            )
        )
    }
    for load in row_loads:
        load.start()
    for load in loads.values():
        load.start()

    barrier = pltpu.get_barrier_semaphore()

    def greet(ctx, tp):
        pl.semaphore_signal(barrier, inc=1, device_id=(ctx, tp), device_id_type=MESH)

    greet(c, partner)

    @pl.when(e > 0)
    def _():
        greet(c, t - 2)

    @pl.when(e < experts - 1)
    def _():
        greet(c, t + 2)

    greeted = 1 + (e > 0).astype(jnp.int32) + (e < experts - 1).astype(jnp.int32)
    for o in range(1, reach + 1):

        @pl.when(c >= o)
        def _():
            greet(c - o, t)
            greet(c - o, partner)

        @pl.when(c + o < ctx_size)
        def _():
            greet(c + o, t)
            greet(c + o, partner)

        greeted += 2 * (c >= o).astype(jnp.int32) + 2 * (c + o < ctx_size).astype(jnp.int32)
    pl.semaphore_wait(barrier, greeted)

    def row_copy(way, src_e, k):
        to = t + 2 if way == 0 else t - 2
        return pltpu.make_async_remote_copy(
            src_ref=rows.at[src_e, :, cut(k)],
            dst_ref=rows.at[src_e, :, cut(k)],
            send_sem=row_send_sem.at[way, src_e, k],
            recv_sem=row_recv_sem.at[src_e, k],
            device_id=(c, to),
            device_id_type=MESH,
        )

    whole = ((0, width),)
    pieces = tuple((k * piece, piece) for k in range(chunks))

    def parts_at(step):
        return pieces if step == experts - 1 else whole

    def y_copy(src_e, part):
        first, count = part
        return pltpu.make_async_remote_copy(
            src_ref=y_send.at[src_e, :, pl.ds(first, count)],
            dst_ref=y_recv.at[src_e, :, pl.ds(first, count)],
            send_sem=y_send_sem.at[src_e, first // piece],
            recv_sem=y_recv_sem.at[src_e, first // piece],
            device_id=(c, partner),
            device_id_type=MESH,
        )

    def kv_copy(o):
        return pltpu.make_async_remote_copy(
            src_ref=kv.at[0],
            dst_ref=kv.at[o],
            send_sem=kv_send_sem.at[o],
            recv_sem=kv_recv_sem.at[o],
            device_id=(c + o, t),
            device_id_type=MESH,
        )

    def part_copy(o, which):
        return pltpu.make_async_remote_copy(
            src_ref=part_send.at[o, which],
            dst_ref=part_recv.at[o, which],
            send_sem=part_send_sem.at[o, which],
            recv_sem=part_recv_sem.at[o, which],
            device_id=(c - o, t if which == 0 else partner),
            device_id_type=MESH,
        )

    for k in range(chunks):
        row_loads[k].wait()

        @pl.when(e < experts - 1)
        def _():
            row_copy(0, e, k).start()

        @pl.when(e > 0)
        def _():
            row_copy(1, e, k).start()

    loads["k"].wait()
    loads["v"].wait()
    for o in range(1, reach + 1):

        @pl.when(c + o < ctx_size)
        def _():
            kv_copy(o).start()

    loads["ids"].wait()
    loads["gates"].wait()
    named = ids[...] == e
    hit = jnp.sum(jnp.where(named, 1.0, 0.0), axis=0, keepdims=True)
    gate = jnp.sum(jnp.where(named, gates[...], 0.0), axis=0, keepdims=True)
    hit = jnp.broadcast_to(hit, (2 * cap, n)).T
    row_i = lax.broadcasted_iota(jnp.int32, (n, n), 0)
    col_i = lax.broadcasted_iota(jnp.int32, (n, n), 1)
    before = jnp.where(col_i < row_i, 1.0, 0.0).astype(BF16)
    rank = dot(before, hit.astype(BF16), ((1,), (0,)))
    slot = lax.broadcasted_iota(jnp.int32, (n, 2 * cap), 1)
    slot = jnp.where(slot < cap, slot + cap * y, slot - cap * y).astype(F32)
    chosen = jnp.where(rank == slot, hit, 0.0)
    chosen = chosen.T
    pick[...] = chosen.astype(BF16)
    slot_gate[...] = jnp.sum(chosen * gate, axis=1, keepdims=True)[:cap]
    gate_acc[...] = jnp.zeros_like(gate_acc)

    def dexp_copy(src, part):
        first, count = part
        cols = pl.ds(pl.multiple_of(src * width + first, HD), count)
        return pltpu.make_async_copy(
            dexp_out.at[:, cols], dexp_hbm.at[0, :, cols], dexp_sem.at[src, first // piece]
        )

    out_copies = [
        pltpu.make_async_copy(source, target, out_sem.at[i])
        for i, (source, target) in enumerate(
            ((dq_out, dq_hbm), (dk_out, dk_hbm), (dv_out, dv_hbm), (dgate_out, dgate_hbm))
        )
    ]

    def finish(src, part, routed):
        first, count = part
        cols = pl.ds(pl.multiple_of(src * width + first, HD), count)
        product = routed * eo[:, cols].astype(F32)
        total = gate_acc[...]
        for i in range(count // HD):
            total += product[:, i * HD : (i + 1) * HD]
        gate_acc[...] = total
        dexp_out[:, cols] = (slot_gate[...] * routed).astype(BF16)
        dexp_copy(src, part).start()

    def take(src_e, part):
        first, count = part
        cols = pl.ds(first, count)
        picked = dot(pick[...], rows[src_e, :, cols], ((1,), (0,)))
        y_send[src_e, :, cols] = picked[cap:].astype(BF16)
        y_copy(src_e, part).start()
        finish(src_e * 2 + y, part, picked[:cap])

    def take_other(src_e, part):
        first, count = part
        y_copy(src_e, part).wait_recv()
        other = y_recv[src_e, :, pl.ds(first, count)]
        finish(src_e * 2 + 1 - y, part, other.astype(F32))

    loads["eo"].wait()
    take(e, whole[0])

    loads["q"].wait()
    loads["do"].wait()
    loads["o"].wait()
    loads["docs"].wait()
    for h in range(QH_DEV):
        at, cols = slice(h * n, (h + 1) * n), slice(h * HD, (h + 1) * HD)
        query, grad, output = q_raw[:, cols], do_raw[:, cols], o_raw[:, cols]
        q_s[at] = query
        do_s[at] = grad
        query, grad = query.astype(F32), grad.astype(F32)
        delta[at] = jnp.sum(grad * output.astype(F32), axis=1, keepdims=True)
        q_half[at] = jnp.where(y == 0, query, pltpu.roll(query, HD // 2, 1)).astype(BF16)
        do_half[at] = jnp.where(y == 1, grad, pltpu.roll(grad, HD // 2, 1)).astype(BF16)

    q_docs = jnp.broadcast_to(docs[pl.ds(c, 1), :].astype(F32), (n, n)).T
    score_max[...] = jnp.full_like(score_max, -1e30)
    score_sum[...] = jnp.zeros_like(score_sum)
    dq_acc[...] = jnp.zeros_like(dq_acc)

    def scores_of(o):
        k_docs = docs[pl.ds(jnp.maximum(c - o, 0), 1), :].astype(F32)
        allowed = (k_docs == q_docs) & (col_i - o * n <= row_i) & (c >= o)
        s = dot(q_s[...], kv[o, 0], ((1,), (1,))) * scaling
        s = jnp.where(jnp.concatenate([allowed] * QH_DEV, axis=0), s, -1e30)
        score[o] = s
        score_max[...] = jnp.maximum(score_max[...], s)

    for o in range(1, reach + 1):

        @pl.when(c >= o)
        def _():
            kv_copy(o).wait_recv()

        @pl.when(c < o)
        def _():
            kv[o] = jnp.zeros(kv.shape[1:], BF16)

    each(reach + 1, scores_of)
    row_max = jnp.max(score_max[...], axis=1, keepdims=True)
    score_max[...] = jnp.broadcast_to(row_max, score_max.shape)

    def exp_of(o):
        p = jnp.exp(score[o] - score_max[...])
        score[o] = p
        score_sum[...] += p

    each(reach + 1, exp_of)
    inverse = 1.0 / jnp.sum(score_sum[...], axis=1, keepdims=True)
    score_sum[...] = jnp.broadcast_to(inverse, score_sum.shape)
    low = lax.broadcasted_iota(jnp.int32, (n, HD), 1) < HD // 2

    def grads_of(o):
        probs = score[o] * score_sum[...]
        prob_grad = dot(do_s[...], kv[o, 1], ((1,), (1,)))
        score_grad = (probs * (prob_grad - delta[...])).astype(BF16)
        dq_acc[...] += dot(score_grad, kv[o, 0], ((1,), (0,)))
        dk = dot(score_grad, q_half[...], ((0,), (0,))) * scaling
        dv = dot(probs.astype(BF16), do_half[...], ((0,), (0,)))
        own = jnp.where(low, dk, dv)
        part_send[o, 1] = jnp.where(low, dv, dk).astype(BF16)
        if isinstance(o, int) and o == 0:
            part_own[...] = own
        else:
            part_send[o, 0] = own.astype(BF16)

    def send_parts(o):
        @pl.when(c >= o)
        def _():
            part_copy(o, 0).start()
            part_copy(o, 1).start()

    def forward(step, k):
        for way, src_e, present in sources(step):

            @pl.when(present)
            def _():
                row_copy(way, src_e, k).wait_recv()

                @pl.when(e < experts - 1 if way == 0 else e > 0)
                def _():
                    row_copy(way, src_e, k).start()

    def sources(step):
        return ((0, e - step, e >= step), (1, e + step, e + step < experts))

    early = 0
    if reach <= 3:
        while early < chunks - 1:
            forward(1, early)
            early += 1
        late = list(range(reach, reach // 2, -1))
        for o in late:
            grads_of(o)
        for o in late:
            send_parts(o)
        while early < chunks:
            forward(1, early)
            early += 1
        near = list(range(reach // 2, -1, -1))
        for o in near:
            grads_of(o)
        for o in near[:-1]:
            send_parts(o)
    else:

        @pl.loop(0, reach)
        def _(i):
            grads_of(reach - i)
            send_parts(reach - i)

        grads_of(0)
    part_copy(0, 1).start()
    for h in range(QH_DEV):
        dq_out[:, h * HD : (h + 1) * HD] = (dq_acc[h * n : (h + 1) * n] * scaling).astype(BF16)
    out_copies[0].start()

    def arrive(step):
        todo = parts_at(step)
        for k in range(chunks):
            if step > 1 or k >= early:
                forward(step, k)
            if len(todo) == 1 and k < chunks - 1:
                continue
            for _way, src_e, present in sources(step):

                @pl.when(present)
                def _():
                    take(src_e, todo[min(k, len(todo) - 1)])

    def arrive_other(step):
        if step == 0:
            take_other(e, whole[0])
            return
        for part in parts_at(step):
            for _way, src_e, present in sources(step):

                @pl.when(present)
                def _():
                    take_other(src_e, part)

    def sum_parts():
        part_copy(0, 1).wait_recv()
        part_own[...] += pltpu.roll(part_recv[0, 1].astype(F32), HD // 2, 1)
        for o in range(1, reach + 1):

            @pl.when(c + o < ctx_size)
            def _():
                part_copy(o, 0).wait_recv()
                part_copy(o, 1).wait_recv()
                part_own[...] += part_recv[o, 0].astype(F32) + pltpu.roll(
                    part_recv[o, 1].astype(F32), HD // 2, 1
                )

        summed = part_own[...].T.astype(BF16)
        dk_out[...] = summed[: HD // 2]
        dv_out[...] = summed[HD // 2 :]
        out_copies[1].start()
        out_copies[2].start()

    for step in range(1, experts):
        arrive(step)
        arrive_other(step - 1)
        if step == max(1, experts - 2):
            sum_parts()
    arrive_other(experts - 1)

    gate_sum = jnp.sum(gate_acc[...], axis=1, keepdims=True)
    dgate_out[...] = jnp.broadcast_to(gate_sum, (cap, HD)).T[:1]
    out_copies[3].start()

    y_copy(e, whole[0]).wait_send()
    dexp_copy(e * 2, whole[0]).wait()
    dexp_copy(e * 2 + 1, whole[0]).wait()
    for k in range(chunks):

        @pl.when(e < experts - 1)
        def _():
            row_copy(0, e, k).wait_send()

        @pl.when(e > 0)
        def _():
            row_copy(1, e, k).wait_send()

    for step in range(1, experts):
        for way, src_e, present in sources(step):

            @pl.when(present)
            def _():
                for part in parts_at(step):
                    y_copy(src_e, part).wait_send()
                    dexp_copy(src_e * 2, part).wait()
                    dexp_copy(src_e * 2 + 1, part).wait()

                @pl.when(e < experts - 1 if way == 0 else e > 0)
                def _():
                    for k in range(chunks):
                        row_copy(way, src_e, k).wait_send()

    for copy in out_copies:
        copy.wait()
    part_copy(0, 1).wait_send()
    for o in range(1, reach + 1):

        @pl.when(c + o < ctx_size)
        def _():
            kv_copy(o).wait_send()

        @pl.when(c >= o)
        def _():
            part_copy(o, 0).wait_send()
            part_copy(o, 1).wait_send()


def write(*refs):
    sources, targets, held, sem = refs[:5], refs[5:10], refs[10:15], refs[15]
    into = [
        pltpu.make_async_copy(source, hold, sem.at[0, i])
        for i, (source, hold) in enumerate(zip(sources, held))
    ]
    out = [
        pltpu.make_async_copy(hold, target, sem.at[1, i])
        for i, (hold, target) in enumerate(zip(held, targets))
    ]
    for copy in into:
        copy.start()
    for first, second in zip(into, out):
        first.wait()
        second.start()
    for copy in out:
        copy.wait()


def local(
    queries,
    key_rows,
    value_rows,
    out_grad,
    attn_out,
    doc_ids,
    row_grad,
    gate_weights,
    expert_ids,
    expert_out,
):
    ctx_size, tp_size = lax.axis_size("ctx"), lax.axis_size("tp")
    n, width = row_grad.shape
    cap, features = expert_out.shape[1:]
    experts = tp_size // 2
    reach = min((doc_ids.shape[0] // 2 + n) // n, ctx_size - 1)
    chunks = 2 if width % (2 * HD) == 0 else 1
    blocks = reach + 1
    stacked = QH_DEV * n
    dma = pltpu.SemaphoreType.DMA
    out_shape = (
        jax.ShapeDtypeStruct(queries.shape, BF16),
        jax.ShapeDtypeStruct((HD // 2, n), BF16),
        jax.ShapeDtypeStruct((HD // 2, n), BF16),
        jax.ShapeDtypeStruct((1, cap), F32),
        jax.ShapeDtypeStruct(expert_out.shape, BF16),
    )
    outs = pl.pallas_call(
        functools.partial(kernel, ctx_size, tp_size, reach, chunks),
        out_shape=out_shape,
        in_specs=[pl.BlockSpec(memory_space=pltpu.HBM)] * 10,
        out_specs=[pl.BlockSpec(memory_space=pltpu.HBM)] * 5,
        scratch_shapes=[
            *(pltpu.VMEM(out.shape, out.dtype) for out in out_shape[:4]),
            pltpu.VMEM((cap, features), BF16),
            pltpu.VMEM(queries.shape, BF16),
            pltpu.VMEM(queries.shape, BF16),
            pltpu.VMEM(queries.shape, BF16),
            pltpu.VMEM((doc_ids.shape[0] // n, n), jnp.int32),
            pltpu.VMEM(gate_weights.shape[::-1], F32),
            pltpu.VMEM(expert_ids.shape[::-1], jnp.int32),
            pltpu.VMEM((cap, features), BF16),
            pltpu.VMEM((blocks, 2, n, HD), BF16),
            pltpu.VMEM((stacked, HD), BF16),
            pltpu.VMEM((stacked, HD), BF16),
            pltpu.VMEM((stacked, HD), BF16),
            pltpu.VMEM((stacked, HD), BF16),
            pltpu.VMEM((stacked, 1), F32),
            pltpu.VMEM((blocks, stacked, n), F32),
            pltpu.VMEM((stacked, n), F32),
            pltpu.VMEM((stacked, n), F32),
            pltpu.VMEM((stacked, HD), F32),
            pltpu.VMEM((blocks, 2, n, HD), BF16),
            pltpu.VMEM((n, HD), F32),
            pltpu.VMEM((blocks, 2, n, HD), BF16),
            pltpu.VMEM((experts, n, width), BF16),
            pltpu.VMEM((2 * cap, n), BF16),
            pltpu.VMEM((cap, 1), F32),
            pltpu.VMEM((experts, cap, width), BF16),
            pltpu.VMEM((experts, cap, width), BF16),
            pltpu.VMEM((cap, HD), F32),
            dma((9,)),
            dma((chunks,)),
            dma((blocks,)),
            dma((blocks,)),
            dma((blocks, 2)),
            dma((blocks, 2)),
            dma((2, experts, chunks)),
            dma((experts, chunks)),
            dma((experts, chunks)),
            dma((experts, chunks)),
            dma((4,)),
            dma((tp_size, chunks)),
        ],
        compiler_params=pltpu.CompilerParams(
            collective_id=0, has_side_effects=True, vmem_limit_bytes=VMEM
        ),
        name="backward",
    )(
        queries,
        key_rows,
        value_rows,
        out_grad,
        attn_out,
        doc_ids.reshape(-1, n),
        row_grad,
        gate_weights.T,
        expert_ids.T,
        expert_out,
    )
    query_grad, key_grad, value_grad, gate_grad, expert_grad = pl.pallas_call(
        write,
        out_shape=out_shape,
        in_specs=[pl.BlockSpec(memory_space=pltpu.HBM)] * 5,
        out_specs=[pl.BlockSpec(memory_space=pltpu.HBM)] * 5,
        scratch_shapes=[
            *(pltpu.VMEM(out.shape, out.dtype) for out in out_shape),
            dma((2, 5)),
        ],
        compiler_params=pltpu.CompilerParams(vmem_limit_bytes=VMEM),
        name="write",
    )(*outs)
    return (query_grad, key_grad.T, value_grad.T, gate_grad, expert_grad)


def solution(mesh):
    in_specs = (
        P("ctx", "tp"),
        P("ctx", None),
        P("ctx", None),
        P("ctx", "tp"),
        P("ctx", "tp"),
        P(),
        P("ctx", "tp"),
        P("ctx", None),
        P("ctx", None),
        P("ctx", "tp", None),
    )
    out_specs = (
        P("ctx", "tp"),
        P("ctx", "tp"),
        P("ctx", "tp"),
        P("ctx", "tp"),
        P("ctx", "tp", None),
    )
    return jax.shard_map(local, mesh=mesh, in_specs=in_specs, out_specs=out_specs, check_vma=False)
```

```python
import functools
import math

import jax
import jax.numpy as jnp
from jax import lax
from jax.experimental import pallas as pl
from jax.experimental.pallas import tpu as pltpu
from jax.sharding import PartitionSpec as P

HD = 128
QH_DEV = 3
F32 = jnp.float32
BF16 = jnp.bfloat16
MESH = pl.DeviceIdType.MESH
VMEM = 62 * 1024 * 1024


def dot(a, b, dims):
    return lax.dot_general(a, b, (dims, ((), ())), preferred_element_type=F32)


def each(count, body):
    if count <= 4:
        for i in range(count):
            body(i)
    else:
        lax.fori_loop(0, count, lambda i, _: (body(i), 0)[1], 0)


def kernel(
    ctx_size,
    tp_size,
    reach,
    chunks,
    q_in,
    k_in,
    v_in,
    do_in,
    o_in,
    docs_in,
    rows_in,
    gates_in,
    ids_in,
    eo_in,
    dq_hbm,
    dk_hbm,
    dv_hbm,
    dgate_hbm,
    dexp_hbm,
    dq_out,
    dk_out,
    dv_out,
    dgate_out,
    dexp_out,
    q_raw,
    do_raw,
    o_raw,
    docs,
    gates,
    ids,
    eo,
    kv,
    q_s,
    q_half,
    do_s,
    do_half,
    delta,
    score,
    score_max,
    score_sum,
    dq_acc,
    part_send,
    part_own,
    part_recv,
    rows,
    pick,
    slot_gate,
    y_send,
    y_recv,
    gate_acc,
    in_sem,
    rows_in_sem,
    kv_send_sem,
    kv_recv_sem,
    part_send_sem,
    part_recv_sem,
    row_send_sem,
    row_recv_sem,
    y_send_sem,
    y_recv_sem,
    out_sem,
    dexp_sem,
):
    c = lax.axis_index("ctx")
    t = lax.axis_index("tp")
    e, y = t // 2, t % 2
    partner = e * 2 + 1 - y
    experts = tp_size // 2
    n = q_in.shape[0]
    cap = eo.shape[0]
    width = rows_in.shape[1]
    piece = width // chunks
    scaling = 1.0 / math.sqrt(HD)
    head_cols = pl.ds(pl.multiple_of(e * HD, HD), HD)

    def cut(k):
        return pl.ds(k * piece, piece)

    row_loads = [
        pltpu.make_async_copy(
            rows_in.at[:, cut(k)], rows.at[e, :, cut(k)], rows_in_sem.at[k]
        )
        for k in range(chunks)
    ]
    loads = {
        name: pltpu.make_async_copy(src, dst, in_sem.at[i])
        for i, (name, src, dst) in enumerate(
            (
                ("k", k_in.at[:, head_cols], kv.at[0, 0]),
                ("v", v_in.at[:, head_cols], kv.at[0, 1]),
                ("ids", ids_in, ids),
                ("gates", gates_in, gates),
                ("q", q_in, q_raw),
                ("do", do_in, do_raw),
                ("o", o_in, o_raw),
                ("docs", docs_in, docs),
                ("eo", eo_in.at[0], eo),
            )
        )
    }
    for load in row_loads:
        load.start()
    for load in loads.values():
        load.start()

    barrier = pltpu.get_barrier_semaphore()

    def greet(ctx, tp):
        pl.semaphore_signal(barrier, inc=1, device_id=(ctx, tp), device_id_type=MESH)

    greet(c, partner)

    @pl.when(e > 0)
    def _():
        greet(c, t - 2)

    @pl.when(e < experts - 1)
    def _():
        greet(c, t + 2)

    greeted = 1 + (e > 0).astype(jnp.int32) + (e < experts - 1).astype(jnp.int32)
    for o in range(1, reach + 1):

        @pl.when(c >= o)
        def _():
            greet(c - o, t)
            greet(c - o, partner)

        @pl.when(c + o < ctx_size)
        def _():
            greet(c + o, t)
            greet(c + o, partner)

        greeted += 2 * (c >= o).astype(jnp.int32) + 2 * (c + o < ctx_size).astype(jnp.int32)
    pl.semaphore_wait(barrier, greeted)

    def row_copy(way, src_e, k):
        to = t + 2 if way == 0 else t - 2
        return pltpu.make_async_remote_copy(
            src_ref=rows.at[src_e, :, cut(k)],
            dst_ref=rows.at[src_e, :, cut(k)],
            send_sem=row_send_sem.at[way, src_e, k],
            recv_sem=row_recv_sem.at[src_e, k],
            device_id=(c, to),
            device_id_type=MESH,
        )

    whole = ((0, width),)
    pieces = tuple((k * piece, piece) for k in range(chunks))

    def parts_at(step):
        return pieces if step == experts - 1 else whole

    def y_copy(src_e, part):
        first, count = part
        return pltpu.make_async_remote_copy(
            src_ref=y_send.at[src_e, :, pl.ds(first, count)],
            dst_ref=y_recv.at[src_e, :, pl.ds(first, count)],
            send_sem=y_send_sem.at[src_e, first // piece],
            recv_sem=y_recv_sem.at[src_e, first // piece],
            device_id=(c, partner),
            device_id_type=MESH,
        )

    def kv_copy(o):
        return pltpu.make_async_remote_copy(
            src_ref=kv.at[0],
            dst_ref=kv.at[o],
            send_sem=kv_send_sem.at[o],
            recv_sem=kv_recv_sem.at[o],
            device_id=(c + o, t),
            device_id_type=MESH,
        )

    def part_copy(o, which):
        return pltpu.make_async_remote_copy(
            src_ref=part_send.at[o, which],
            dst_ref=part_recv.at[o, which],
            send_sem=part_send_sem.at[o, which],
            recv_sem=part_recv_sem.at[o, which],
            device_id=(c - o, t if which == 0 else partner),
            device_id_type=MESH,
        )

    for k in range(chunks):
        row_loads[k].wait()

        @pl.when(e < experts - 1)
        def _():
            row_copy(0, e, k).start()

        @pl.when(e > 0)
        def _():
            row_copy(1, e, k).start()

    loads["k"].wait()
    loads["v"].wait()
    for o in range(1, reach + 1):

        @pl.when(c + o < ctx_size)
        def _():
            kv_copy(o).start()

    loads["ids"].wait()
    loads["gates"].wait()
    named = ids[...] == e
    hit = jnp.sum(jnp.where(named, 1.0, 0.0), axis=0, keepdims=True)
    gate = jnp.sum(jnp.where(named, gates[...], 0.0), axis=0, keepdims=True)
    hit = jnp.broadcast_to(hit, (2 * cap, n)).T
    row_i = lax.broadcasted_iota(jnp.int32, (n, n), 0)
    col_i = lax.broadcasted_iota(jnp.int32, (n, n), 1)
    before = jnp.where(col_i < row_i, 1.0, 0.0).astype(BF16)
    rank = dot(before, hit.astype(BF16), ((1,), (0,)))
    slot = lax.broadcasted_iota(jnp.int32, (n, 2 * cap), 1)
    slot = jnp.where(slot < cap, slot + cap * y, slot - cap * y).astype(F32)
    chosen = jnp.where(rank == slot, hit, 0.0)
    chosen = chosen.T
    pick[...] = chosen.astype(BF16)
    slot_gate[...] = jnp.sum(chosen * gate, axis=1, keepdims=True)[:cap]
    gate_acc[...] = jnp.zeros_like(gate_acc)

    def dexp_copy(src, part):
        first, count = part
        cols = pl.ds(pl.multiple_of(src * width + first, HD), count)
        return pltpu.make_async_copy(
            dexp_out.at[:, cols], dexp_hbm.at[0, :, cols], dexp_sem.at[src, first // piece]
        )

    out_copies = [
        pltpu.make_async_copy(source, target, out_sem.at[i])
        for i, (source, target) in enumerate(
            ((dq_out, dq_hbm), (dk_out, dk_hbm), (dv_out, dv_hbm), (dgate_out, dgate_hbm))
        )
    ]

    def finish(src, part, routed):
        first, count = part
        cols = pl.ds(pl.multiple_of(src * width + first, HD), count)
        product = routed * eo[:, cols].astype(F32)
        total = gate_acc[...]
        for i in range(count // HD):
            total += product[:, i * HD : (i + 1) * HD]
        gate_acc[...] = total
        dexp_out[:, cols] = (slot_gate[...] * routed).astype(BF16)
        dexp_copy(src, part).start()

    def take(src_e, part):
        first, count = part
        cols = pl.ds(first, count)
        picked = dot(pick[...], rows[src_e, :, cols], ((1,), (0,)))
        y_send[src_e, :, cols] = picked[cap:].astype(BF16)
        y_copy(src_e, part).start()
        finish(src_e * 2 + y, part, picked[:cap])

    def take_other(src_e, part):
        first, count = part
        y_copy(src_e, part).wait_recv()
        other = y_recv[src_e, :, pl.ds(first, count)]
        finish(src_e * 2 + 1 - y, part, other.astype(F32))

    loads["eo"].wait()
    take(e, whole[0])

    loads["q"].wait()
    loads["do"].wait()
    loads["o"].wait()
    loads["docs"].wait()
    for h in range(QH_DEV):
        at, cols = slice(h * n, (h + 1) * n), slice(h * HD, (h + 1) * HD)
        query, grad, output = q_raw[:, cols], do_raw[:, cols], o_raw[:, cols]
        q_s[at] = query
        do_s[at] = grad
        query, grad = query.astype(F32), grad.astype(F32)
        delta[at] = jnp.sum(grad * output.astype(F32), axis=1, keepdims=True)
        q_half[at] = jnp.where(y == 0, query, pltpu.roll(query, HD // 2, 1)).astype(BF16)
        do_half[at] = jnp.where(y == 1, grad, pltpu.roll(grad, HD // 2, 1)).astype(BF16)

    q_docs = jnp.broadcast_to(docs[pl.ds(c, 1), :].astype(F32), (n, n)).T
    score_max[...] = jnp.full_like(score_max, -1e30)
    score_sum[...] = jnp.zeros_like(score_sum)
    dq_acc[...] = jnp.zeros_like(dq_acc)

    def scores_of(o):
        k_docs = docs[pl.ds(jnp.maximum(c - o, 0), 1), :].astype(F32)
        allowed = (k_docs == q_docs) & (col_i - o * n <= row_i) & (c >= o)
        s = dot(q_s[...], kv[o, 0], ((1,), (1,))) * scaling
        s = jnp.where(jnp.concatenate([allowed] * QH_DEV, axis=0), s, -1e30)
        score[o] = s
        score_max[...] = jnp.maximum(score_max[...], s)

    for o in range(1, reach + 1):

        @pl.when(c >= o)
        def _():
            kv_copy(o).wait_recv()

        @pl.when(c < o)
        def _():
            kv[o] = jnp.zeros(kv.shape[1:], BF16)

    each(reach + 1, scores_of)
    row_max = jnp.max(score_max[...], axis=1, keepdims=True)
    score_max[...] = jnp.broadcast_to(row_max, score_max.shape)

    def exp_of(o):
        p = jnp.exp(score[o] - score_max[...])
        score[o] = p
        score_sum[...] += p

    each(reach + 1, exp_of)
    inverse = 1.0 / jnp.sum(score_sum[...], axis=1, keepdims=True)
    score_sum[...] = jnp.broadcast_to(inverse, score_sum.shape)
    low = lax.broadcasted_iota(jnp.int32, (n, HD), 1) < HD // 2

    def grads_of(o):
        probs = score[o] * score_sum[...]
        prob_grad = dot(do_s[...], kv[o, 1], ((1,), (1,)))
        score_grad = (probs * (prob_grad - delta[...])).astype(BF16)
        dq_acc[...] += dot(score_grad, kv[o, 0], ((1,), (0,)))
        dk = dot(score_grad, q_half[...], ((0,), (0,))) * scaling
        dv = dot(probs.astype(BF16), do_half[...], ((0,), (0,)))
        own = jnp.where(low, dk, dv)
        part_send[o, 1] = jnp.where(low, dv, dk).astype(BF16)
        if isinstance(o, int) and o == 0:
            part_own[...] = own
        else:
            part_send[o, 0] = own.astype(BF16)

    def send_parts(o):
        @pl.when(c >= o)
        def _():
            part_copy(o, 0).start()
            part_copy(o, 1).start()

    def forward(step, k):
        if step >= experts:
            return
        for way, src_e, present in sources(step):

            @pl.when(jnp.logical_and(present, passes(way)))
            def _():
                row_copy(way, src_e, k).wait_recv()
                row_copy(way, src_e, k).start()

    def passes(way):
        return e < experts - 1 if way == 0 else e > 0

    def sources(step):
        return ((0, e - step, e >= step), (1, e + step, e + step < experts))

    if reach <= 3:
        late = list(range(reach, reach // 2, -1))
        near = list(range(reach // 2, -1, -1))
        forward(1, 0)
        for o in late:
            grads_of(o)
        for o in late:
            send_parts(o)
        for k in range(1, chunks):
            forward(1, k)
        for o in near:
            grads_of(o)
        for o in near[:-1]:
            send_parts(o)
    else:
        for k in range(chunks):
            forward(1, k)

        @pl.loop(0, reach)
        def _(i):
            grads_of(reach - i)
            send_parts(reach - i)

        grads_of(0)
    part_copy(0, 1).start()
    for h in range(QH_DEV):
        dq_out[:, h * HD : (h + 1) * HD] = (dq_acc[h * n : (h + 1) * n] * scaling).astype(BF16)
    out_copies[0].start()

    def arrive(step):
        for part in parts_at(step):
            for way, src_e, present in sources(step):

                @pl.when(jnp.logical_and(present, jnp.logical_not(passes(way))))
                def _():
                    for k in range(chunks):
                        if part[0] <= k * piece < part[0] + part[1]:
                            row_copy(way, src_e, k).wait_recv()

                @pl.when(present)
                def _():
                    take(src_e, part)

    def arrive_other(step):
        if step == 0:
            take_other(e, whole[0])
            return
        for part in parts_at(step):
            for _way, src_e, present in sources(step):

                @pl.when(present)
                def _():
                    take_other(src_e, part)

    def sum_parts():
        part_copy(0, 1).wait_recv()
        part_own[...] += pltpu.roll(part_recv[0, 1].astype(F32), HD // 2, 1)
        for o in range(1, reach + 1):

            @pl.when(c + o < ctx_size)
            def _():
                part_copy(o, 0).wait_recv()
                part_copy(o, 1).wait_recv()
                part_own[...] += part_recv[o, 0].astype(F32) + pltpu.roll(
                    part_recv[o, 1].astype(F32), HD // 2, 1
                )

        summed = part_own[...].T.astype(BF16)
        dk_out[...] = summed[: HD // 2]
        dv_out[...] = summed[HD // 2 :]
        out_copies[1].start()
        out_copies[2].start()

    for step in range(1, experts):
        forward(step + 1, 0)
        arrive(step)
        for k in range(1, chunks):
            forward(step + 1, k)
        arrive_other(step - 1)
        if step == max(1, experts - 2):
            sum_parts()
    arrive_other(experts - 1)

    gate_sum = jnp.sum(gate_acc[...], axis=1, keepdims=True)
    dgate_out[...] = jnp.broadcast_to(gate_sum, (cap, HD)).T[:1]
    out_copies[3].start()

    y_copy(e, whole[0]).wait_send()
    dexp_copy(e * 2, whole[0]).wait()
    dexp_copy(e * 2 + 1, whole[0]).wait()
    for k in range(chunks):

        @pl.when(e < experts - 1)
        def _():
            row_copy(0, e, k).wait_send()

        @pl.when(e > 0)
        def _():
            row_copy(1, e, k).wait_send()

    for step in range(1, experts):
        for way, src_e, present in sources(step):

            @pl.when(present)
            def _():
                for part in parts_at(step):
                    y_copy(src_e, part).wait_send()
                    dexp_copy(src_e * 2, part).wait()
                    dexp_copy(src_e * 2 + 1, part).wait()

                @pl.when(e < experts - 1 if way == 0 else e > 0)
                def _():
                    for k in range(chunks):
                        row_copy(way, src_e, k).wait_send()

    for copy in out_copies:
        copy.wait()
    part_copy(0, 1).wait_send()
    for o in range(1, reach + 1):

        @pl.when(c + o < ctx_size)
        def _():
            kv_copy(o).wait_send()

        @pl.when(c >= o)
        def _():
            part_copy(o, 0).wait_send()
            part_copy(o, 1).wait_send()


def write(*refs):
    sources, targets, held, sem = refs[:5], refs[5:10], refs[10:15], refs[15]
    into, out = [], []

    def through(source, hold, target):
        i = len(into)
        into.append(pltpu.make_async_copy(source, hold, sem.at[0, i]))
        out.append(pltpu.make_async_copy(hold, target, sem.at[1, i]))

    for source, target, hold in zip(sources, targets, held):
        if len(source.shape) == 2:
            through(source, hold, target)
            continue
        for row in range(0, source.shape[1], 16):
            at = pl.ds(row, 16)
            through(source.at[0, at], hold.at[0, at], target.at[0, at])
    for copy in into:
        copy.start()
    for first, second in zip(into, out):
        first.wait()
        second.start()
    for copy in out:
        copy.wait()


def local(
    queries,
    key_rows,
    value_rows,
    out_grad,
    attn_out,
    doc_ids,
    row_grad,
    gate_weights,
    expert_ids,
    expert_out,
):
    ctx_size, tp_size = lax.axis_size("ctx"), lax.axis_size("tp")
    n, width = row_grad.shape
    cap, features = expert_out.shape[1:]
    experts = tp_size // 2
    reach = min((doc_ids.shape[0] // 2 + n) // n, ctx_size - 1)
    chunks = 2 if width % (2 * HD) == 0 else 1
    blocks = reach + 1
    stacked = QH_DEV * n
    dma = pltpu.SemaphoreType.DMA
    out_shape = (
        jax.ShapeDtypeStruct(queries.shape, BF16),
        jax.ShapeDtypeStruct((HD // 2, n), BF16),
        jax.ShapeDtypeStruct((HD // 2, n), BF16),
        jax.ShapeDtypeStruct((1, cap), F32),
        jax.ShapeDtypeStruct(expert_out.shape, BF16),
    )
    outs = pl.pallas_call(
        functools.partial(kernel, ctx_size, tp_size, reach, chunks),
        out_shape=out_shape,
        in_specs=[pl.BlockSpec(memory_space=pltpu.HBM)] * 10,
        out_specs=[pl.BlockSpec(memory_space=pltpu.HBM)] * 5,
        scratch_shapes=[
            *(pltpu.VMEM(out.shape, out.dtype) for out in out_shape[:4]),
            pltpu.VMEM((cap, features), BF16),
            pltpu.VMEM(queries.shape, BF16),
            pltpu.VMEM(queries.shape, BF16),
            pltpu.VMEM(queries.shape, BF16),
            pltpu.VMEM((doc_ids.shape[0] // n, n), jnp.int32),
            pltpu.VMEM(gate_weights.shape[::-1], F32),
            pltpu.VMEM(expert_ids.shape[::-1], jnp.int32),
            pltpu.VMEM((cap, features), BF16),
            pltpu.VMEM((blocks, 2, n, HD), BF16),
            pltpu.VMEM((stacked, HD), BF16),
            pltpu.VMEM((stacked, HD), BF16),
            pltpu.VMEM((stacked, HD), BF16),
            pltpu.VMEM((stacked, HD), BF16),
            pltpu.VMEM((stacked, 1), F32),
            pltpu.VMEM((blocks, stacked, n), F32),
            pltpu.VMEM((stacked, n), F32),
            pltpu.VMEM((stacked, n), F32),
            pltpu.VMEM((stacked, HD), F32),
            pltpu.VMEM((blocks, 2, n, HD), BF16),
            pltpu.VMEM((n, HD), F32),
            pltpu.VMEM((blocks, 2, n, HD), BF16),
            pltpu.VMEM((experts, n, width), BF16),
            pltpu.VMEM((2 * cap, n), BF16),
            pltpu.VMEM((cap, 1), F32),
            pltpu.VMEM((experts, cap, width), BF16),
            pltpu.VMEM((experts, cap, width), BF16),
            pltpu.VMEM((cap, HD), F32),
            dma((9,)),
            dma((chunks,)),
            dma((blocks,)),
            dma((blocks,)),
            dma((blocks, 2)),
            dma((blocks, 2)),
            dma((2, experts, chunks)),
            dma((experts, chunks)),
            dma((experts, chunks)),
            dma((experts, chunks)),
            dma((4,)),
            dma((tp_size, chunks)),
        ],
        compiler_params=pltpu.CompilerParams(
            collective_id=0, has_side_effects=True, vmem_limit_bytes=VMEM
        ),
        name="backward",
    )(
        queries,
        key_rows,
        value_rows,
        out_grad,
        attn_out,
        doc_ids.reshape(-1, n),
        row_grad,
        gate_weights.T,
        expert_ids.T,
        expert_out,
    )
    query_grad, key_grad, value_grad, gate_grad, expert_grad = pl.pallas_call(
        write,
        out_shape=out_shape,
        in_specs=[pl.BlockSpec(memory_space=pltpu.HBM)] * 5,
        out_specs=[pl.BlockSpec(memory_space=pltpu.HBM)] * 5,
        scratch_shapes=[
            *(pltpu.VMEM(out.shape, out.dtype) for out in out_shape),
            dma((2, 4 + cap // 16)),
        ],
        compiler_params=pltpu.CompilerParams(vmem_limit_bytes=VMEM),
        name="write",
    )(*outs)
    return (query_grad, key_grad.T, value_grad.T, gate_grad, expert_grad)


def solution(mesh):
    in_specs = (
        P("ctx", "tp"),
        P("ctx", None),
        P("ctx", None),
        P("ctx", "tp"),
        P("ctx", "tp"),
        P(),
        P("ctx", "tp"),
        P("ctx", None),
        P("ctx", None),
        P("ctx", "tp", None),
    )
    out_specs = (
        P("ctx", "tp"),
        P("ctx", "tp"),
        P("ctx", "tp"),
        P("ctx", "tp"),
        P("ctx", "tp", None),
    )
    return jax.shard_map(local, mesh=mesh, in_specs=in_specs, out_specs=out_specs, check_vma=False)
```

```python
import functools
import math

import jax
import jax.numpy as jnp
from jax import lax
from jax.experimental import pallas as pl
from jax.experimental.pallas import tpu as pltpu
from jax.sharding import PartitionSpec as P

HD = 128
QH_DEV = 3
F32 = jnp.float32
BF16 = jnp.bfloat16
MESH = pl.DeviceIdType.MESH
VMEM = 40 * 1024 * 1024


def dot(a, b, dims):
    return lax.dot_general(a, b, (dims, ((), ())), preferred_element_type=F32)


def each(count, body):
    if count <= 4:
        for i in range(count):
            body(i)
    else:
        lax.fori_loop(0, count, lambda i, _: (body(i), 0)[1], 0)


def cuts(width):
    pieces, first, rest = [], 0, width // HD
    while rest > 0:
        count = (rest + 1) // 2
        pieces.append((first * HD, count * HD, len(pieces)))
        first, rest = first + count, rest - count
    return pieces


def kernel(
    ctx_size,
    tp_size,
    reach,
    q_in,
    k_in,
    v_in,
    do_in,
    o_in,
    docs_in,
    rows_in,
    gates_in,
    ids_in,
    eo_in,
    dq_out,
    dk_out,
    dv_out,
    dgate_out,
    dexp_out,
    q_raw,
    do_raw,
    o_raw,
    docs,
    gates,
    ids,
    eo,
    kv,
    q_s,
    q_half,
    do_s,
    do_half,
    delta,
    score,
    score_max,
    score_sum,
    dq_acc,
    part_send,
    part_own,
    part_recv,
    rows,
    pick,
    slot_gate,
    y_send,
    y_recv,
    gate_acc,
    in_sem,
    rows_in_sem,
    kv_send_sem,
    kv_recv_sem,
    part_send_sem,
    part_recv_sem,
    row_send_sem,
    row_recv_sem,
    y_send_sem,
    y_recv_sem,
):
    c = lax.axis_index("ctx")
    t = lax.axis_index("tp")
    e, y = t // 2, t % 2
    partner = e * 2 + 1 - y
    experts = tp_size // 2
    n = q_in.shape[0]
    cap = eo.shape[0]
    width = rows_in.shape[1]
    pieces = cuts(width)
    chunks = len(pieces)
    scaling = 1.0 / math.sqrt(HD)
    head_cols = pl.ds(pl.multiple_of(e * HD, HD), HD)

    def cut(k):
        return pl.ds(*pieces[k][:2])

    row_loads = [
        pltpu.make_async_copy(
            rows_in.at[:, cut(k)], rows.at[e, :, cut(k)], rows_in_sem.at[k]
        )
        for k in range(chunks)
    ]
    loads = {
        name: pltpu.make_async_copy(src, dst, in_sem.at[i])
        for i, (name, src, dst) in enumerate(
            (
                ("k", k_in.at[:, head_cols], kv.at[0, 0]),
                ("v", v_in.at[:, head_cols], kv.at[0, 1]),
                ("ids", ids_in, ids),
                ("gates", gates_in, gates),
                ("q", q_in, q_raw),
                ("do", do_in, do_raw),
                ("o", o_in, o_raw),
                ("docs", docs_in, docs),
                ("eo", eo_in.at[0], eo),
            )
        )
    }
    for load in row_loads:
        load.start()
    for load in loads.values():
        load.start()

    barrier = pltpu.get_barrier_semaphore()

    def greet(ctx, tp):
        pl.semaphore_signal(barrier, inc=1, device_id=(ctx, tp), device_id_type=MESH)

    greet(c, partner)

    @pl.when(e > 0)
    def _():
        greet(c, t - 2)

    @pl.when(e < experts - 1)
    def _():
        greet(c, t + 2)

    greeted = 1 + (e > 0).astype(jnp.int32) + (e < experts - 1).astype(jnp.int32)
    for o in range(1, reach + 1):

        @pl.when(c >= o)
        def _():
            greet(c - o, t)
            greet(c - o, partner)

        @pl.when(c + o < ctx_size)
        def _():
            greet(c + o, t)
            greet(c + o, partner)

        greeted += 2 * (c >= o).astype(jnp.int32) + 2 * (c + o < ctx_size).astype(jnp.int32)
    pl.semaphore_wait(barrier, greeted)

    def row_copy(way, src_e, k):
        to = t + 2 if way == 0 else t - 2
        return pltpu.make_async_remote_copy(
            src_ref=rows.at[src_e, :, cut(k)],
            dst_ref=rows.at[src_e, :, cut(k)],
            send_sem=row_send_sem.at[way, src_e, k],
            recv_sem=row_recv_sem.at[src_e, k],
            device_id=(c, to),
            device_id_type=MESH,
        )

    whole = ((0, width, 0),)

    def parts_at(step):
        return pieces if step == experts - 1 else whole

    def y_copy(src_e, part):
        first, count, index = part
        return pltpu.make_async_remote_copy(
            src_ref=y_send.at[src_e, :, pl.ds(first, count)],
            dst_ref=y_recv.at[src_e, :, pl.ds(first, count)],
            send_sem=y_send_sem.at[src_e, index],
            recv_sem=y_recv_sem.at[src_e, index],
            device_id=(c, partner),
            device_id_type=MESH,
        )

    def kv_copy(o):
        return pltpu.make_async_remote_copy(
            src_ref=kv.at[0],
            dst_ref=kv.at[o],
            send_sem=kv_send_sem.at[o],
            recv_sem=kv_recv_sem.at[o],
            device_id=(c + o, t),
            device_id_type=MESH,
        )

    def part_copy(o, which):
        return pltpu.make_async_remote_copy(
            src_ref=part_send.at[o, which],
            dst_ref=part_recv.at[o, which],
            send_sem=part_send_sem.at[o, which],
            recv_sem=part_recv_sem.at[o, which],
            device_id=(c - o, t if which == 0 else partner),
            device_id_type=MESH,
        )

    for k in range(chunks):
        row_loads[k].wait()

        @pl.when(e < experts - 1)
        def _():
            row_copy(0, e, k).start()

        @pl.when(e > 0)
        def _():
            row_copy(1, e, k).start()

    loads["k"].wait()
    loads["v"].wait()
    for o in range(1, reach + 1):

        @pl.when(c + o < ctx_size)
        def _():
            kv_copy(o).start()

    loads["ids"].wait()
    loads["gates"].wait()
    named = ids[...] == e
    hit = jnp.sum(jnp.where(named, 1.0, 0.0), axis=0, keepdims=True)
    gate = jnp.sum(jnp.where(named, gates[...], 0.0), axis=0, keepdims=True)
    hit = jnp.broadcast_to(hit, (2 * cap, n)).T
    row_i = lax.broadcasted_iota(jnp.int32, (n, n), 0)
    col_i = lax.broadcasted_iota(jnp.int32, (n, n), 1)
    before = jnp.where(col_i < row_i, 1.0, 0.0).astype(BF16)
    rank = dot(before, hit.astype(BF16), ((1,), (0,)))
    slot = lax.broadcasted_iota(jnp.int32, (n, 2 * cap), 1)
    slot = jnp.where(slot < cap, slot + cap * y, slot - cap * y).astype(F32)
    chosen = jnp.where(rank == slot, hit, 0.0)
    chosen = chosen.T
    pick[...] = chosen.astype(BF16)
    slot_gate[...] = jnp.sum(chosen * gate, axis=1, keepdims=True)[:cap]
    gate_acc[...] = jnp.zeros_like(gate_acc)

    def finish(src, part, routed):
        first, count, _ = part
        cols = pl.ds(pl.multiple_of(src * width + first, HD), count)
        product = routed * eo[:, cols].astype(F32)
        total = gate_acc[...]
        for i in range(count // HD):
            total += product[:, i * HD : (i + 1) * HD]
        gate_acc[...] = total
        dexp_out[0, :, cols] = (slot_gate[...] * routed).astype(BF16)

    def take(src_e, part):
        first, count, index = part
        cols = pl.ds(first, count)
        picked = dot(pick[...], rows[src_e, :, cols], ((1,), (0,)))
        y_send[src_e, :, cols] = picked[cap:].astype(BF16)
        y_copy(src_e, part).start()
        finish(src_e * 2 + y, part, picked[:cap])

    def take_other(src_e, part):
        first, count, index = part
        y_copy(src_e, part).wait_recv()
        other = y_recv[src_e, :, pl.ds(first, count)]
        finish(src_e * 2 + 1 - y, part, other.astype(F32))

    loads["eo"].wait()
    take(e, whole[0])

    loads["q"].wait()
    loads["do"].wait()
    loads["o"].wait()
    loads["docs"].wait()
    for h in range(QH_DEV):
        at, cols = slice(h * n, (h + 1) * n), slice(h * HD, (h + 1) * HD)
        query, grad, output = q_raw[:, cols], do_raw[:, cols], o_raw[:, cols]
        q_s[at] = query
        do_s[at] = grad
        query, grad = query.astype(F32), grad.astype(F32)
        delta[at] = jnp.sum(grad * output.astype(F32), axis=1, keepdims=True)
        q_half[at] = jnp.where(y == 0, query, pltpu.roll(query, HD // 2, 1)).astype(BF16)
        do_half[at] = jnp.where(y == 1, grad, pltpu.roll(grad, HD // 2, 1)).astype(BF16)

    q_docs = jnp.broadcast_to(docs[pl.ds(c, 1), :].astype(F32), (n, n)).T
    score_max[...] = jnp.full_like(score_max, -1e30)
    score_sum[...] = jnp.zeros_like(score_sum)
    dq_acc[...] = jnp.zeros_like(dq_acc)

    def scores_of(o):
        k_docs = docs[pl.ds(jnp.maximum(c - o, 0), 1), :].astype(F32)
        allowed = (k_docs == q_docs) & (col_i - o * n <= row_i) & (c >= o)
        s = dot(q_s[...], kv[o, 0], ((1,), (1,))) * scaling
        s = jnp.where(jnp.concatenate([allowed] * QH_DEV, axis=0), s, -1e30)
        score[o] = s
        score_max[...] = jnp.maximum(score_max[...], s)

    for o in range(1, reach + 1):

        @pl.when(c >= o)
        def _():
            kv_copy(o).wait_recv()

        @pl.when(c < o)
        def _():
            kv[o] = jnp.zeros(kv.shape[1:], BF16)

    each(reach + 1, scores_of)
    row_max = jnp.max(score_max[...], axis=1, keepdims=True)
    score_max[...] = jnp.broadcast_to(row_max, score_max.shape)

    def exp_of(o):
        p = jnp.exp(score[o] - score_max[...])
        score[o] = p
        score_sum[...] += p

    each(reach + 1, exp_of)
    inverse = 1.0 / jnp.sum(score_sum[...], axis=1, keepdims=True)
    score_sum[...] = jnp.broadcast_to(inverse, score_sum.shape)
    low = lax.broadcasted_iota(jnp.int32, (n, HD), 1) < HD // 2

    def grads_of(o):
        probs = score[o] * score_sum[...]
        prob_grad = dot(do_s[...], kv[o, 1], ((1,), (1,)))
        score_grad = (probs * (prob_grad - delta[...])).astype(BF16)
        dq_acc[...] += dot(score_grad, kv[o, 0], ((1,), (0,)))
        dk = dot(score_grad, q_half[...], ((0,), (0,))) * scaling
        dv = dot(probs.astype(BF16), do_half[...], ((0,), (0,)))
        own = jnp.where(low, dk, dv)
        part_send[o, 1] = jnp.where(low, dv, dk).astype(BF16)
        if isinstance(o, int) and o == 0:
            part_own[...] = own
        else:
            part_send[o, 0] = own.astype(BF16)

    def send_parts(o):
        @pl.when(c >= o)
        def _():
            part_copy(o, 0).start()
            part_copy(o, 1).start()

    def forward(step, k):
        if step >= experts:
            return
        for way, src_e, present in sources(step):

            @pl.when(jnp.logical_and(present, passes(way)))
            def _():
                row_copy(way, src_e, k).wait_recv()
                row_copy(way, src_e, k).start()

    def passes(way):
        return e < experts - 1 if way == 0 else e > 0

    def sources(step):
        return ((0, e - step, e >= step), (1, e + step, e + step < experts))

    if reach <= 3:
        late = list(range(reach, reach // 2, -1))
        near = list(range(reach // 2, -1, -1))
        forward(1, 0)
        for o in late:
            grads_of(o)
        for o in late:
            send_parts(o)
        for k in range(1, chunks):
            forward(1, k)
        for o in near:
            grads_of(o)
        for o in near[:-1]:
            send_parts(o)
    else:
        for k in range(chunks):
            forward(1, k)

        @pl.loop(0, reach)
        def _(i):
            grads_of(reach - i)
            send_parts(reach - i)

        grads_of(0)
    part_copy(0, 1).start()
    for h in range(QH_DEV):
        dq_out[:, h * HD : (h + 1) * HD] = (dq_acc[h * n : (h + 1) * n] * scaling).astype(BF16)

    def arrive(step):
        for part in parts_at(step):
            for way, src_e, present in sources(step):

                @pl.when(jnp.logical_and(present, jnp.logical_not(passes(way))))
                def _():
                    for k in range(chunks):
                        if part[0] <= pieces[k][0] < part[0] + part[1]:
                            row_copy(way, src_e, k).wait_recv()

                @pl.when(present)
                def _():
                    take(src_e, part)

    def arrive_other(step):
        if step == 0:
            take_other(e, whole[0])
            return
        for part in parts_at(step):
            for _way, src_e, present in sources(step):

                @pl.when(present)
                def _():
                    take_other(src_e, part)

    def sum_parts():
        part_copy(0, 1).wait_recv()
        part_own[...] += pltpu.roll(part_recv[0, 1].astype(F32), HD // 2, 1)
        for o in range(1, reach + 1):

            @pl.when(c + o < ctx_size)
            def _():
                part_copy(o, 0).wait_recv()
                part_copy(o, 1).wait_recv()
                part_own[...] += part_recv[o, 0].astype(F32) + pltpu.roll(
                    part_recv[o, 1].astype(F32), HD // 2, 1
                )

        summed = part_own[...].T.astype(BF16)
        dk_out[...] = summed[: HD // 2]
        dv_out[...] = summed[HD // 2 :]

    for step in range(1, experts):
        forward(step + 1, 0)
        arrive(step)
        for k in range(1, chunks):
            forward(step + 1, k)
        arrive_other(step - 1)
        if step == max(1, experts - 2):
            sum_parts()
    arrive_other(experts - 1)

    gate_sum = jnp.sum(gate_acc[...], axis=1, keepdims=True)
    dgate_out[...] = jnp.broadcast_to(gate_sum, (cap, HD)).T[:1]

    y_copy(e, whole[0]).wait_send()
    for k in range(chunks):

        @pl.when(e < experts - 1)
        def _():
            row_copy(0, e, k).wait_send()

        @pl.when(e > 0)
        def _():
            row_copy(1, e, k).wait_send()

    for step in range(1, experts):
        for way, src_e, present in sources(step):

            @pl.when(present)
            def _():
                for part in parts_at(step):
                    y_copy(src_e, part).wait_send()

                @pl.when(e < experts - 1 if way == 0 else e > 0)
                def _():
                    for k in range(chunks):
                        row_copy(way, src_e, k).wait_send()

    part_copy(0, 1).wait_send()
    for o in range(1, reach + 1):

        @pl.when(c + o < ctx_size)
        def _():
            kv_copy(o).wait_send()

        @pl.when(c >= o)
        def _():
            part_copy(o, 0).wait_send()
            part_copy(o, 1).wait_send()


def write(*refs):
    sources, targets, sem = refs[:5], refs[5:10], refs[10]
    copies = [
        pltpu.make_async_copy(source, target, sem.at[i])
        for i, (source, target) in enumerate(zip(sources, targets))
    ]
    for copy in reversed(copies):
        copy.start()
    for copy in copies:
        copy.wait()


def local(
    queries,
    key_rows,
    value_rows,
    out_grad,
    attn_out,
    doc_ids,
    row_grad,
    gate_weights,
    expert_ids,
    expert_out,
):
    ctx_size, tp_size = lax.axis_size("ctx"), lax.axis_size("tp")
    n, width = row_grad.shape
    cap, features = expert_out.shape[1:]
    experts = tp_size // 2
    reach = min((doc_ids.shape[0] // 2 + n) // n, ctx_size - 1)
    chunks = len(cuts(width))
    blocks = reach + 1
    stacked = QH_DEV * n
    dma = pltpu.SemaphoreType.DMA
    out_shape = (
        jax.ShapeDtypeStruct(queries.shape, BF16),
        jax.ShapeDtypeStruct((HD // 2, n), BF16),
        jax.ShapeDtypeStruct((HD // 2, n), BF16),
        jax.ShapeDtypeStruct((1, cap), F32),
        jax.ShapeDtypeStruct(expert_out.shape, BF16),
    )
    outs = pl.pallas_call(
        functools.partial(kernel, ctx_size, tp_size, reach),
        out_shape=tuple(pltpu.VMEM(out.shape, out.dtype) for out in out_shape),
        in_specs=[pl.BlockSpec(memory_space=pltpu.HBM)] * 10,
        out_specs=[pl.BlockSpec(memory_space=pltpu.VMEM)] * 5,
        scratch_shapes=[
            pltpu.VMEM(queries.shape, BF16),
            pltpu.VMEM(queries.shape, BF16),
            pltpu.VMEM(queries.shape, BF16),
            pltpu.VMEM((doc_ids.shape[0] // n, n), jnp.int32),
            pltpu.VMEM(gate_weights.shape[::-1], F32),
            pltpu.VMEM(expert_ids.shape[::-1], jnp.int32),
            pltpu.VMEM((cap, features), BF16),
            pltpu.VMEM((blocks, 2, n, HD), BF16),
            pltpu.VMEM((stacked, HD), BF16),
            pltpu.VMEM((stacked, HD), BF16),
            pltpu.VMEM((stacked, HD), BF16),
            pltpu.VMEM((stacked, HD), BF16),
            pltpu.VMEM((stacked, 1), F32),
            pltpu.VMEM((blocks, stacked, n), F32),
            pltpu.VMEM((stacked, n), F32),
            pltpu.VMEM((stacked, n), F32),
            pltpu.VMEM((stacked, HD), F32),
            pltpu.VMEM((blocks, 2, n, HD), BF16),
            pltpu.VMEM((n, HD), F32),
            pltpu.VMEM((blocks, 2, n, HD), BF16),
            pltpu.VMEM((experts, n, width), BF16),
            pltpu.VMEM((2 * cap, n), BF16),
            pltpu.VMEM((cap, 1), F32),
            pltpu.VMEM((experts, cap, width), BF16),
            pltpu.VMEM((experts, cap, width), BF16),
            pltpu.VMEM((cap, HD), F32),
            dma((9,)),
            dma((chunks,)),
            dma((blocks,)),
            dma((blocks,)),
            dma((blocks, 2)),
            dma((blocks, 2)),
            dma((2, experts, chunks)),
            dma((experts, chunks)),
            dma((experts, chunks)),
            dma((experts, chunks)),
        ],
        compiler_params=pltpu.CompilerParams(
            collective_id=0, has_side_effects=True, vmem_limit_bytes=VMEM
        ),
        name="backward",
    )(
        *(
            pltpu.with_memory_space_constraint(operand, pltpu.HBM)
            for operand in (
                queries,
                key_rows,
                value_rows,
                out_grad,
                attn_out,
                doc_ids.reshape(-1, n),
                row_grad,
                gate_weights.T,
                expert_ids.T,
                expert_out,
            )
        )
    )
    query_grad, key_grad, value_grad, gate_grad, expert_grad = pl.pallas_call(
        write,
        out_shape=out_shape,
        in_specs=[pl.BlockSpec(memory_space=pltpu.VMEM)] * 5,
        out_specs=[pl.BlockSpec(memory_space=pltpu.HBM)] * 5,
        scratch_shapes=[dma((5,))],
        name="write",
    )(*outs)
    return (query_grad, key_grad.T, value_grad.T, gate_grad, expert_grad)


def solution(mesh):
    in_specs = (
        P("ctx", "tp"),
        P("ctx", None),
        P("ctx", None),
        P("ctx", "tp"),
        P("ctx", "tp"),
        P(),
        P("ctx", "tp"),
        P("ctx", None),
        P("ctx", None),
        P("ctx", "tp", None),
    )
    out_specs = (
        P("ctx", "tp"),
        P("ctx", "tp"),
        P("ctx", "tp"),
        P("ctx", "tp"),
        P("ctx", "tp", None),
    )
    return jax.shard_map(local, mesh=mesh, in_specs=in_specs, out_specs=out_specs, check_vma=False)
```

```python
import functools
import math

import jax
import jax.numpy as jnp
from jax import lax
from jax.experimental import pallas as pl
from jax.experimental.pallas import tpu as pltpu
from jax.sharding import PartitionSpec as P

HD = 128
QH_DEV = 3
F32 = jnp.float32
BF16 = jnp.bfloat16
MESH = pl.DeviceIdType.MESH
VMEM = 40 * 1024 * 1024


def dot(a, b, dims):
    return lax.dot_general(a, b, (dims, ((), ())), preferred_element_type=F32)


def each(count, body):
    if count <= 4:
        for i in range(count):
            body(i)
    else:
        lax.fori_loop(0, count, lambda i, _: (body(i), 0)[1], 0)


def cuts(width):
    pieces, first, rest = [], 0, width // HD
    while rest > 0:
        count = (rest + 1) // 2
        pieces.append((first * HD, count * HD, len(pieces)))
        first, rest = first + count, rest - count
    return pieces


def kernel(
    ctx_size,
    tp_size,
    reach,
    q_in,
    k_in,
    v_in,
    do_in,
    o_in,
    docs_in,
    rows_in,
    gates_in,
    ids_in,
    eo_in,
    dq_out,
    dk_out,
    dv_out,
    dgate_out,
    dexp_out,
    q_raw,
    do_raw,
    o_raw,
    docs,
    gates,
    ids,
    eo,
    kv,
    q_s,
    q_half,
    do_s,
    do_half,
    delta,
    score,
    score_max,
    score_sum,
    dq_acc,
    part_send,
    part_own,
    part_recv,
    rows,
    pick,
    slot_gate,
    y_send,
    y_recv,
    gate_acc,
    in_sem,
    rows_in_sem,
    kv_send_sem,
    kv_recv_sem,
    part_send_sem,
    part_recv_sem,
    row_send_sem,
    row_recv_sem,
    y_send_sem,
    y_recv_sem,
):
    c = lax.axis_index("ctx")
    t = lax.axis_index("tp")
    e, y = t // 2, t % 2
    partner = e * 2 + 1 - y
    experts = tp_size // 2
    n = q_in.shape[0]
    cap = eo.shape[0]
    width = rows_in.shape[1]
    pieces = cuts(width)
    chunks = len(pieces)
    scaling = 1.0 / math.sqrt(HD)
    head_cols = pl.ds(pl.multiple_of(e * HD, HD), HD)

    def cut(k):
        return pl.ds(*pieces[k][:2])

    row_loads = [
        pltpu.make_async_copy(
            rows_in.at[:, cut(k)], rows.at[e, :, cut(k)], rows_in_sem.at[k]
        )
        for k in range(chunks)
    ]
    loads = {
        name: pltpu.make_async_copy(src, dst, in_sem.at[i])
        for i, (name, src, dst) in enumerate(
            (
                ("k", k_in.at[:, head_cols], kv.at[0, 0]),
                ("v", v_in.at[:, head_cols], kv.at[0, 1]),
                ("ids", ids_in, ids),
                ("gates", gates_in, gates),
                ("q", q_in, q_raw),
                ("do", do_in, do_raw),
                ("o", o_in, o_raw),
                ("docs", docs_in, docs),
                ("eo", eo_in.at[0], eo),
            )
        )
    }
    for load in row_loads:
        load.start()
    for load in loads.values():
        load.start()

    barrier = pltpu.get_barrier_semaphore()

    def greet(ctx, tp):
        pl.semaphore_signal(barrier, inc=1, device_id=(ctx, tp), device_id_type=MESH)

    greet(c, partner)

    @pl.when(e > 0)
    def _():
        greet(c, t - 2)

    @pl.when(e < experts - 1)
    def _():
        greet(c, t + 2)

    greeted = 1 + (e > 0).astype(jnp.int32) + (e < experts - 1).astype(jnp.int32)
    for o in range(1, reach + 1):

        @pl.when(c >= o)
        def _():
            greet(c - o, t)
            greet(c - o, partner)

        @pl.when(c + o < ctx_size)
        def _():
            greet(c + o, t)
            greet(c + o, partner)

        greeted += 2 * (c >= o).astype(jnp.int32) + 2 * (c + o < ctx_size).astype(jnp.int32)
    pl.semaphore_wait(barrier, greeted)

    def row_copy(way, src_e, k):
        to = t + 2 if way == 0 else t - 2
        return pltpu.make_async_remote_copy(
            src_ref=rows.at[src_e, :, cut(k)],
            dst_ref=rows.at[src_e, :, cut(k)],
            send_sem=row_send_sem.at[way, src_e, k],
            recv_sem=row_recv_sem.at[src_e, k],
            device_id=(c, to),
            device_id_type=MESH,
        )

    whole = ((0, width, 0),)

    def parts_at(step):
        return pieces if step == experts - 1 else whole

    def y_copy(src_e, part):
        first, count, index = part
        return pltpu.make_async_remote_copy(
            src_ref=y_send.at[src_e, :, pl.ds(first, count)],
            dst_ref=y_recv.at[src_e, :, pl.ds(first, count)],
            send_sem=y_send_sem.at[src_e, index],
            recv_sem=y_recv_sem.at[src_e, index],
            device_id=(c, partner),
            device_id_type=MESH,
        )

    def kv_copy(o):
        return pltpu.make_async_remote_copy(
            src_ref=kv.at[0],
            dst_ref=kv.at[o],
            send_sem=kv_send_sem.at[o],
            recv_sem=kv_recv_sem.at[o],
            device_id=(c + o, t),
            device_id_type=MESH,
        )

    def part_copy(o, which):
        return pltpu.make_async_remote_copy(
            src_ref=part_send.at[o, which],
            dst_ref=part_recv.at[o, which],
            send_sem=part_send_sem.at[o, which],
            recv_sem=part_recv_sem.at[o, which],
            device_id=(c - o, t if which == 0 else partner),
            device_id_type=MESH,
        )

    for k in range(chunks):
        row_loads[k].wait()

        @pl.when(e < experts - 1)
        def _():
            row_copy(0, e, k).start()

        @pl.when(e > 0)
        def _():
            row_copy(1, e, k).start()

    loads["k"].wait()
    loads["v"].wait()
    for o in range(1, reach + 1):

        @pl.when(c + o < ctx_size)
        def _():
            kv_copy(o).start()

    loads["ids"].wait()
    loads["gates"].wait()
    named = ids[...] == e
    hit = jnp.sum(jnp.where(named, 1.0, 0.0), axis=0, keepdims=True)
    gate = jnp.sum(jnp.where(named, gates[...], 0.0), axis=0, keepdims=True)
    hit = jnp.broadcast_to(hit, (2 * cap, n)).T
    row_i = lax.broadcasted_iota(jnp.int32, (n, n), 0)
    col_i = lax.broadcasted_iota(jnp.int32, (n, n), 1)
    before = jnp.where(col_i < row_i, 1.0, 0.0).astype(BF16)
    rank = dot(before, hit.astype(BF16), ((1,), (0,)))
    slot = lax.broadcasted_iota(jnp.int32, (n, 2 * cap), 1)
    slot = jnp.where(slot < cap, slot + cap * y, slot - cap * y).astype(F32)
    chosen = jnp.where(rank == slot, hit, 0.0)
    chosen = chosen.T
    pick[...] = chosen.astype(BF16)
    slot_gate[...] = jnp.sum(chosen * gate, axis=1, keepdims=True)[:cap]
    gate_acc[...] = jnp.zeros_like(gate_acc)

    def finish(src, part, routed):
        first, count, _ = part
        cols = pl.ds(pl.multiple_of(src * width + first, HD), count)
        product = routed * eo[:, cols].astype(F32)
        total = gate_acc[...]
        for i in range(count // HD):
            total += product[:, i * HD : (i + 1) * HD]
        gate_acc[...] = total
        dexp_out[0, :, cols] = (slot_gate[...] * routed).astype(BF16)

    def take(src_e, part):
        first, count, index = part
        cols = pl.ds(first, count)
        picked = dot(pick[...], rows[src_e, :, cols], ((1,), (0,)))
        y_send[src_e, :, cols] = picked[cap:].astype(BF16)
        y_copy(src_e, part).start()
        finish(src_e * 2 + y, part, picked[:cap])

    def take_other(src_e, part):
        first, count, index = part
        y_copy(src_e, part).wait_recv()
        other = y_recv[src_e, :, pl.ds(first, count)]
        finish(src_e * 2 + 1 - y, part, other.astype(F32))

    loads["eo"].wait()
    take(e, whole[0])

    loads["q"].wait()
    loads["do"].wait()
    loads["o"].wait()
    loads["docs"].wait()
    for h in range(QH_DEV):
        at, cols = slice(h * n, (h + 1) * n), slice(h * HD, (h + 1) * HD)
        query, grad, output = q_raw[:, cols], do_raw[:, cols], o_raw[:, cols]
        q_s[at] = query
        do_s[at] = grad
        query, grad = query.astype(F32), grad.astype(F32)
        delta[at] = jnp.sum(grad * output.astype(F32), axis=1, keepdims=True)
        q_half[at] = jnp.where(y == 0, query, pltpu.roll(query, HD // 2, 1)).astype(BF16)
        do_half[at] = jnp.where(y == 1, grad, pltpu.roll(grad, HD // 2, 1)).astype(BF16)

    q_docs = jnp.broadcast_to(docs[pl.ds(c, 1), :].astype(F32), (n, n)).T
    score_max[...] = jnp.full_like(score_max, -1e30)
    score_sum[...] = jnp.zeros_like(score_sum)
    dq_acc[...] = jnp.zeros_like(dq_acc)

    def scores_of(o):
        k_docs = docs[pl.ds(jnp.maximum(c - o, 0), 1), :].astype(F32)
        allowed = (k_docs == q_docs) & (col_i - o * n <= row_i) & (c >= o)
        s = dot(q_s[...], kv[o, 0], ((1,), (1,))) * scaling
        s = jnp.where(jnp.concatenate([allowed] * QH_DEV, axis=0), s, -1e30)
        score[o] = s
        score_max[...] = jnp.maximum(score_max[...], s)

    for o in range(1, reach + 1):

        @pl.when(c >= o)
        def _():
            kv_copy(o).wait_recv()

        @pl.when(c < o)
        def _():
            kv[o] = jnp.zeros(kv.shape[1:], BF16)

    each(reach + 1, scores_of)
    row_max = jnp.max(score_max[...], axis=1, keepdims=True)
    score_max[...] = jnp.broadcast_to(row_max, score_max.shape)

    def exp_of(o):
        p = jnp.exp(score[o] - score_max[...])
        score[o] = p
        score_sum[...] += p

    each(reach + 1, exp_of)
    inverse = 1.0 / jnp.sum(score_sum[...], axis=1, keepdims=True)
    score_sum[...] = jnp.broadcast_to(inverse, score_sum.shape)
    low = lax.broadcasted_iota(jnp.int32, (n, HD), 1) < HD // 2

    def grads_of(o):
        probs = score[o] * score_sum[...]
        prob_grad = dot(do_s[...], kv[o, 1], ((1,), (1,)))
        score_grad = (probs * (prob_grad - delta[...])).astype(BF16)
        dq_acc[...] += dot(score_grad, kv[o, 0], ((1,), (0,)))
        dk = dot(score_grad, q_half[...], ((0,), (0,))) * scaling
        dv = dot(probs.astype(BF16), do_half[...], ((0,), (0,)))
        own = jnp.where(low, dk, dv)
        part_send[o, 1] = jnp.where(low, dv, dk).astype(BF16)
        if isinstance(o, int) and o == 0:
            part_own[...] = own
        else:
            part_send[o, 0] = own.astype(BF16)

    def send_parts(o):
        @pl.when(c >= o)
        def _():
            part_copy(o, 0).start()
            part_copy(o, 1).start()

    def forward(step, k):
        if step >= experts:
            return
        for way, src_e, present in sources(step):

            @pl.when(jnp.logical_and(present, passes(way)))
            def _():
                row_copy(way, src_e, k).wait_recv()
                row_copy(way, src_e, k).start()

    def passes(way):
        return e < experts - 1 if way == 0 else e > 0

    def sources(step):
        return ((0, e - step, e >= step), (1, e + step, e + step < experts))

    if reach <= 3:
        late = list(range(reach, reach // 2, -1))
        near = list(range(reach // 2, -1, -1))
        forward(1, 0)
        for o in late:
            grads_of(o)
        for o in late:
            send_parts(o)
        for k in range(1, chunks):
            forward(1, k)
        for o in near:
            grads_of(o)
        for o in near[:-1]:
            send_parts(o)
    else:
        for k in range(chunks):
            forward(1, k)

        @pl.loop(0, reach)
        def _(i):
            grads_of(reach - i)
            send_parts(reach - i)

        grads_of(0)
    part_copy(0, 1).start()
    for h in range(QH_DEV):
        dq_out[:, h * HD : (h + 1) * HD] = (dq_acc[h * n : (h + 1) * n] * scaling).astype(BF16)

    def arrive(step):
        for part in parts_at(step):
            for way, src_e, present in sources(step):

                @pl.when(jnp.logical_and(present, jnp.logical_not(passes(way))))
                def _():
                    for k in range(chunks):
                        if part[0] <= pieces[k][0] < part[0] + part[1]:
                            row_copy(way, src_e, k).wait_recv()

                @pl.when(present)
                def _():
                    take(src_e, part)

    def arrive_other(step):
        if step == 0:
            take_other(e, whole[0])
            return
        for part in parts_at(step):
            for _way, src_e, present in sources(step):

                @pl.when(present)
                def _():
                    take_other(src_e, part)

    def sum_parts():
        part_copy(0, 1).wait_recv()
        part_own[...] += pltpu.roll(part_recv[0, 1].astype(F32), HD // 2, 1)
        for o in range(1, reach + 1):

            @pl.when(c + o < ctx_size)
            def _():
                part_copy(o, 0).wait_recv()
                part_copy(o, 1).wait_recv()
                part_own[...] += part_recv[o, 0].astype(F32) + pltpu.roll(
                    part_recv[o, 1].astype(F32), HD // 2, 1
                )

        summed = part_own[...].T.astype(BF16)
        dk_out[...] = summed[: HD // 2]
        dv_out[...] = summed[HD // 2 :]

    for step in range(1, experts):
        forward(step + 1, 0)
        arrive(step)
        for k in range(1, chunks):
            forward(step + 1, k)
        arrive_other(step - 1)
        if step == max(1, experts - 2):
            sum_parts()
    arrive_other(experts - 1)

    gate_sum = jnp.sum(gate_acc[...], axis=1, keepdims=True)
    dgate_out[...] = jnp.broadcast_to(gate_sum, (cap, HD)).T[:1]

    y_copy(e, whole[0]).wait_send()
    for k in range(chunks):

        @pl.when(e < experts - 1)
        def _():
            row_copy(0, e, k).wait_send()

        @pl.when(e > 0)
        def _():
            row_copy(1, e, k).wait_send()

    for step in range(1, experts):
        for way, src_e, present in sources(step):

            @pl.when(present)
            def _():
                for part in parts_at(step):
                    y_copy(src_e, part).wait_send()

                @pl.when(e < experts - 1 if way == 0 else e > 0)
                def _():
                    for k in range(chunks):
                        row_copy(way, src_e, k).wait_send()

    part_copy(0, 1).wait_send()
    for o in range(1, reach + 1):

        @pl.when(c + o < ctx_size)
        def _():
            kv_copy(o).wait_send()

        @pl.when(c >= o)
        def _():
            part_copy(o, 0).wait_send()
            part_copy(o, 1).wait_send()


def write(*refs):
    sources, targets, sem = refs[:5], refs[5:10], refs[10]
    copies = [
        pltpu.make_async_copy(source, target, sem.at[i])
        for i, (source, target) in enumerate(zip(sources, targets))
    ]
    for copy in reversed(copies):
        copy.start()
    for copy in copies:
        copy.wait()


def local(
    queries,
    key_rows,
    value_rows,
    out_grad,
    attn_out,
    doc_ids,
    row_grad,
    gate_weights,
    expert_ids,
    expert_out,
):
    ctx_size, tp_size = lax.axis_size("ctx"), lax.axis_size("tp")
    n, width = row_grad.shape
    cap, features = expert_out.shape[1:]
    experts = tp_size // 2
    reach = min((doc_ids.shape[0] // 2 + n) // n, ctx_size - 1)
    chunks = len(cuts(width))
    blocks = reach + 1
    stacked = QH_DEV * n
    dma = pltpu.SemaphoreType.DMA
    out_shape = (
        jax.ShapeDtypeStruct(queries.shape, BF16),
        jax.ShapeDtypeStruct((HD // 2, n), BF16),
        jax.ShapeDtypeStruct((HD // 2, n), BF16),
        jax.ShapeDtypeStruct((1, cap), F32),
        jax.ShapeDtypeStruct(expert_out.shape, BF16),
    )
    outs = pl.pallas_call(
        functools.partial(kernel, ctx_size, tp_size, reach),
        out_shape=tuple(pltpu.VMEM(out.shape, out.dtype) for out in out_shape),
        in_specs=[pl.BlockSpec(memory_space=pltpu.HBM)] * 10,
        out_specs=[pl.BlockSpec(memory_space=pltpu.VMEM)] * 5,
        scratch_shapes=[
            pltpu.VMEM(queries.shape, BF16),
            pltpu.VMEM(queries.shape, BF16),
            pltpu.VMEM(queries.shape, BF16),
            pltpu.VMEM((doc_ids.shape[0] // n, n), jnp.int32),
            pltpu.VMEM(gate_weights.shape[::-1], F32),
            pltpu.VMEM(expert_ids.shape[::-1], jnp.int32),
            pltpu.VMEM((cap, features), BF16),
            pltpu.VMEM((blocks, 2, n, HD), BF16),
            pltpu.VMEM((stacked, HD), BF16),
            pltpu.VMEM((stacked, HD), BF16),
            pltpu.VMEM((stacked, HD), BF16),
            pltpu.VMEM((stacked, HD), BF16),
            pltpu.VMEM((stacked, 1), F32),
            pltpu.VMEM((blocks, stacked, n), F32),
            pltpu.VMEM((stacked, n), F32),
            pltpu.VMEM((stacked, n), F32),
            pltpu.VMEM((stacked, HD), F32),
            pltpu.VMEM((blocks, 2, n, HD), BF16),
            pltpu.VMEM((n, HD), F32),
            pltpu.VMEM((blocks, 2, n, HD), BF16),
            pltpu.VMEM((experts, n, width), BF16),
            pltpu.VMEM((2 * cap, n), BF16),
            pltpu.VMEM((cap, 1), F32),
            pltpu.VMEM((experts, cap, width), BF16),
            pltpu.VMEM((experts, cap, width), BF16),
            pltpu.VMEM((cap, HD), F32),
            dma((9,)),
            dma((chunks,)),
            dma((blocks,)),
            dma((blocks,)),
            dma((blocks, 2)),
            dma((blocks, 2)),
            dma((2, experts, chunks)),
            dma((experts, chunks)),
            dma((experts, chunks)),
            dma((experts, chunks)),
        ],
        compiler_params=pltpu.CompilerParams(
            collective_id=0, has_side_effects=True, vmem_limit_bytes=VMEM
        ),
        name="backward",
    )(
        *(
            pltpu.with_memory_space_constraint(operand, pltpu.HBM)
            for operand in (
                queries,
                key_rows,
                value_rows,
                out_grad,
                attn_out,
                doc_ids.reshape(-1, n),
                row_grad,
                gate_weights.T,
                expert_ids.T,
                expert_out,
            )
        )
    )
    query_grad, key_grad, value_grad, gate_grad, expert_grad = pl.pallas_call(
        write,
        out_shape=out_shape,
        in_specs=[pl.BlockSpec(memory_space=pltpu.VMEM)] * 5,
        out_specs=[pl.BlockSpec(memory_space=pltpu.HBM)] * 5,
        scratch_shapes=[dma((5,))],
        compiler_params=pltpu.CompilerParams(vmem_limit_bytes=8 * 1024 * 1024),
        name="write",
    )(*outs)
    return (query_grad, key_grad.T, value_grad.T, gate_grad, expert_grad)


def solution(mesh):
    in_specs = (
        P("ctx", "tp"),
        P("ctx", None),
        P("ctx", None),
        P("ctx", "tp"),
        P("ctx", "tp"),
        P(),
        P("ctx", "tp"),
        P("ctx", None),
        P("ctx", None),
        P("ctx", "tp", None),
    )
    out_specs = (
        P("ctx", "tp"),
        P("ctx", "tp"),
        P("ctx", "tp"),
        P("ctx", "tp"),
        P("ctx", "tp", None),
    )
    return jax.shard_map(local, mesh=mesh, in_specs=in_specs, out_specs=out_specs, check_vma=False)
```

```python
import functools
import math

import jax
import jax.numpy as jnp
from jax import lax
from jax.experimental import pallas as pl
from jax.experimental.pallas import tpu as pltpu
from jax.sharding import PartitionSpec as P

HD = 128
QH_DEV = 3
F32 = jnp.float32
BF16 = jnp.bfloat16
MESH = pl.DeviceIdType.MESH
VMEM = 40 * 1024 * 1024


def dot(a, b, dims):
    return lax.dot_general(a, b, (dims, ((), ())), preferred_element_type=F32)


def each(count, body):
    if count <= 4:
        for i in range(count):
            body(i)
    else:
        lax.fori_loop(0, count, lambda i, _: (body(i), 0)[1], 0)


def cuts(width):
    pieces, first, rest = [], 0, width // HD
    while rest > 0:
        count = (rest + 1) // 2
        pieces.append((first * HD, count * HD, len(pieces)))
        first, rest = first + count, rest - count
    return pieces


def kernel(
    ctx_size,
    tp_size,
    reach,
    q_in,
    k_in,
    v_in,
    do_in,
    o_in,
    docs_in,
    rows_in,
    gates_in,
    ids_in,
    eo_in,
    dq_out,
    dk_out,
    dv_out,
    dgate_out,
    dexp_out,
    q_raw,
    do_raw,
    o_raw,
    docs,
    gates,
    ids,
    eo,
    kv,
    q_s,
    q_half,
    do_s,
    do_half,
    delta,
    score,
    score_max,
    score_sum,
    dq_acc,
    part_send,
    part_own,
    part_recv,
    rows,
    pick,
    slot_gate,
    y_send,
    y_recv,
    gate_acc,
    in_sem,
    rows_in_sem,
    kv_send_sem,
    kv_recv_sem,
    part_send_sem,
    part_recv_sem,
    row_send_sem,
    row_recv_sem,
    y_send_sem,
    y_recv_sem,
):
    c = lax.axis_index("ctx")
    t = lax.axis_index("tp")
    e, y = t // 2, t % 2
    partner = e * 2 + 1 - y
    experts = tp_size // 2
    n = q_in.shape[0]
    cap = eo.shape[0]
    width = rows_in.shape[1]
    pieces = cuts(width)
    chunks = len(pieces)
    scaling = 1.0 / math.sqrt(HD)
    head_cols = pl.ds(pl.multiple_of(e * HD, HD), HD)

    def cut(k):
        return pl.ds(*pieces[k][:2])

    row_loads = [
        pltpu.make_async_copy(
            rows_in.at[:, cut(k)], rows.at[e, :, cut(k)], rows_in_sem.at[k]
        )
        for k in range(chunks)
    ]
    loads = {
        name: pltpu.make_async_copy(src, dst, in_sem.at[i])
        for i, (name, src, dst) in enumerate(
            (
                ("k", k_in.at[:, head_cols], kv.at[0, 0]),
                ("v", v_in.at[:, head_cols], kv.at[0, 1]),
                ("ids", ids_in, ids),
                ("gates", gates_in, gates),
                ("q", q_in, q_raw),
                ("do", do_in, do_raw),
                ("o", o_in, o_raw),
                ("docs", docs_in, docs),
                ("eo", eo_in.at[0], eo),
            )
        )
    }
    for load in row_loads:
        load.start()
    for load in loads.values():
        load.start()

    barrier = pltpu.get_barrier_semaphore()

    def greet(ctx, tp):
        pl.semaphore_signal(barrier, inc=1, device_id=(ctx, tp), device_id_type=MESH)

    greet(c, partner)

    @pl.when(e > 0)
    def _():
        greet(c, t - 2)

    @pl.when(e < experts - 1)
    def _():
        greet(c, t + 2)

    greeted = 1 + (e > 0).astype(jnp.int32) + (e < experts - 1).astype(jnp.int32)
    for o in range(1, reach + 1):

        @pl.when(c >= o)
        def _():
            greet(c - o, t)
            greet(c - o, partner)

        @pl.when(c + o < ctx_size)
        def _():
            greet(c + o, t)
            greet(c + o, partner)

        greeted += 2 * (c >= o).astype(jnp.int32) + 2 * (c + o < ctx_size).astype(jnp.int32)
    pl.semaphore_wait(barrier, greeted)

    def row_copy(way, src_e, k):
        to = jnp.minimum(t + 2, tp_size - 1) if way == 0 else jnp.maximum(t - 2, 0)
        return pltpu.make_async_remote_copy(
            src_ref=rows.at[src_e, :, cut(k)],
            dst_ref=rows.at[src_e, :, cut(k)],
            send_sem=row_send_sem.at[way, src_e, k],
            recv_sem=row_recv_sem.at[src_e, k],
            device_id=(c, to),
            device_id_type=MESH,
        )

    whole = ((0, width, 0),)

    def parts_at(step):
        return pieces if step == experts - 1 else whole

    def y_copy(src_e, part):
        first, count, index = part
        return pltpu.make_async_remote_copy(
            src_ref=y_send.at[src_e, :, pl.ds(first, count)],
            dst_ref=y_recv.at[src_e, :, pl.ds(first, count)],
            send_sem=y_send_sem.at[src_e, index],
            recv_sem=y_recv_sem.at[src_e, index],
            device_id=(c, partner),
            device_id_type=MESH,
        )

    def kv_copy(o):
        return pltpu.make_async_remote_copy(
            src_ref=kv.at[0],
            dst_ref=kv.at[o],
            send_sem=kv_send_sem.at[o],
            recv_sem=kv_recv_sem.at[o],
            device_id=(jnp.minimum(c + o, ctx_size - 1), t),
            device_id_type=MESH,
        )

    def part_copy(o, which):
        return pltpu.make_async_remote_copy(
            src_ref=part_send.at[o, which],
            dst_ref=part_recv.at[o, which],
            send_sem=part_send_sem.at[o, which],
            recv_sem=part_recv_sem.at[o, which],
            device_id=(jnp.maximum(c - o, 0), t if which == 0 else partner),
            device_id_type=MESH,
        )

    for k in range(chunks):
        row_loads[k].wait()

        @pl.when(e < experts - 1)
        def _():
            row_copy(0, e, k).start()

        @pl.when(e > 0)
        def _():
            row_copy(1, e, k).start()

    loads["k"].wait()
    loads["v"].wait()
    for o in range(1, reach + 1):

        @pl.when(c + o < ctx_size)
        def _():
            kv_copy(o).start()

    loads["ids"].wait()
    loads["gates"].wait()
    named = ids[...] == e
    hit = jnp.sum(jnp.where(named, 1.0, 0.0), axis=0, keepdims=True)
    gate = jnp.sum(jnp.where(named, gates[...], 0.0), axis=0, keepdims=True)
    hit = jnp.broadcast_to(hit, (2 * cap, n)).T
    row_i = lax.broadcasted_iota(jnp.int32, (n, n), 0)
    col_i = lax.broadcasted_iota(jnp.int32, (n, n), 1)
    before = jnp.where(col_i < row_i, 1.0, 0.0).astype(BF16)
    rank = dot(before, hit.astype(BF16), ((1,), (0,)))
    slot = lax.broadcasted_iota(jnp.int32, (n, 2 * cap), 1)
    slot = jnp.where(slot < cap, slot + cap * y, slot - cap * y).astype(F32)
    chosen = jnp.where(rank == slot, hit, 0.0)
    chosen = chosen.T
    pick[...] = chosen.astype(BF16)
    slot_gate[...] = jnp.sum(chosen * gate, axis=1, keepdims=True)[:cap]
    gate_acc[...] = jnp.zeros_like(gate_acc)

    def finish(src, part, routed):
        first, count, _ = part
        cols = pl.ds(pl.multiple_of(src * width + first, HD), count)
        product = routed * eo[:, cols].astype(F32)
        total = gate_acc[...]
        for i in range(count // HD):
            total += product[:, i * HD : (i + 1) * HD]
        gate_acc[...] = total
        dexp_out[0, :, cols] = (slot_gate[...] * routed).astype(BF16)

    def take(src_e, part):
        first, count, index = part
        cols = pl.ds(first, count)
        picked = dot(pick[...], rows[src_e, :, cols], ((1,), (0,)))
        y_send[src_e, :, cols] = picked[cap:].astype(BF16)
        y_copy(src_e, part).start()
        finish(src_e * 2 + y, part, picked[:cap])

    def take_other(src_e, part):
        first, count, index = part
        y_copy(src_e, part).wait_recv()
        other = y_recv[src_e, :, pl.ds(first, count)]
        finish(src_e * 2 + 1 - y, part, other.astype(F32))

    loads["eo"].wait()
    take(e, whole[0])

    loads["q"].wait()
    loads["do"].wait()
    loads["o"].wait()
    loads["docs"].wait()
    for h in range(QH_DEV):
        at, cols = slice(h * n, (h + 1) * n), slice(h * HD, (h + 1) * HD)
        query, grad, output = q_raw[:, cols], do_raw[:, cols], o_raw[:, cols]
        q_s[at] = query
        do_s[at] = grad
        query, grad = query.astype(F32), grad.astype(F32)
        delta[at] = jnp.sum(grad * output.astype(F32), axis=1, keepdims=True)
        q_half[at] = jnp.where(y == 0, query, pltpu.roll(query, HD // 2, 1)).astype(BF16)
        do_half[at] = jnp.where(y == 1, grad, pltpu.roll(grad, HD // 2, 1)).astype(BF16)

    q_docs = jnp.broadcast_to(docs[pl.ds(c, 1), :].astype(F32), (n, n)).T
    score_max[...] = jnp.full_like(score_max, -1e30)
    score_sum[...] = jnp.zeros_like(score_sum)
    dq_acc[...] = jnp.zeros_like(dq_acc)

    def scores_of(o):
        k_docs = docs[pl.ds(jnp.maximum(c - o, 0), 1), :].astype(F32)
        allowed = (k_docs == q_docs) & (col_i - o * n <= row_i) & (c >= o)
        s = dot(q_s[...], kv[o, 0], ((1,), (1,))) * scaling
        s = jnp.where(jnp.concatenate([allowed] * QH_DEV, axis=0), s, -1e30)
        score[o] = s
        score_max[...] = jnp.maximum(score_max[...], s)

    for o in range(1, reach + 1):

        @pl.when(c >= o)
        def _():
            kv_copy(o).wait_recv()

        @pl.when(c < o)
        def _():
            kv[o] = jnp.zeros(kv.shape[1:], BF16)

    def forward(step, k):
        if step >= experts:
            return
        for way, src_e, present in sources(step):

            @pl.when(jnp.logical_and(present, passes(way)))
            def _():
                row_copy(way, src_e, k).wait_recv()
                row_copy(way, src_e, k).start()

    def passes(way):
        return e < experts - 1 if way == 0 else e > 0

    def sources(step):
        return ((0, e - step, e >= step), (1, e + step, e + step < experts))

    each(reach + 1, scores_of)
    forward(1, 0)
    row_max = jnp.max(score_max[...], axis=1, keepdims=True)
    score_max[...] = jnp.broadcast_to(row_max, score_max.shape)

    def exp_of(o):
        p = jnp.exp(score[o] - score_max[...])
        score[o] = p
        score_sum[...] += p

    each(reach + 1, exp_of)
    inverse = 1.0 / jnp.sum(score_sum[...], axis=1, keepdims=True)
    score_sum[...] = jnp.broadcast_to(inverse, score_sum.shape)
    low = lax.broadcasted_iota(jnp.int32, (n, HD), 1) < HD // 2

    def grads_of(o):
        probs = score[o] * score_sum[...]
        prob_grad = dot(do_s[...], kv[o, 1], ((1,), (1,)))
        score_grad = (probs * (prob_grad - delta[...])).astype(BF16)
        dq_acc[...] += dot(score_grad, kv[o, 0], ((1,), (0,)))
        dk = dot(score_grad, q_half[...], ((0,), (0,))) * scaling
        dv = dot(probs.astype(BF16), do_half[...], ((0,), (0,)))
        own = jnp.where(low, dk, dv)
        part_send[o, 1] = jnp.where(low, dv, dk).astype(BF16)
        if isinstance(o, int) and o == 0:
            part_own[...] = own
        else:
            part_send[o, 0] = own.astype(BF16)

    def send_parts(o):
        @pl.when(c >= o)
        def _():
            part_copy(o, 0).start()
            part_copy(o, 1).start()

    if reach <= 3:
        late = list(range(reach, reach // 2, -1))
        near = list(range(reach // 2, -1, -1))
        for o in late:
            grads_of(o)
        for o in late:
            send_parts(o)
        for k in range(1, chunks):
            forward(1, k)
        for o in near:
            grads_of(o)
        for o in near[:-1]:
            send_parts(o)
    else:
        for k in range(1, chunks):
            forward(1, k)

        @pl.loop(0, reach)
        def _(i):
            grads_of(reach - i)
            send_parts(reach - i)

        grads_of(0)
    part_copy(0, 1).start()
    for h in range(QH_DEV):
        dq_out[:, h * HD : (h + 1) * HD] = (dq_acc[h * n : (h + 1) * n] * scaling).astype(BF16)

    def arrive(step):
        for part in parts_at(step):
            for way, src_e, present in sources(step):

                @pl.when(jnp.logical_and(present, jnp.logical_not(passes(way))))
                def _():
                    for k in range(chunks):
                        if part[0] <= pieces[k][0] < part[0] + part[1]:
                            row_copy(way, src_e, k).wait_recv()

                @pl.when(present)
                def _():
                    take(src_e, part)

    def arrive_other(step):
        if step == 0:
            take_other(e, whole[0])
            return
        for part in parts_at(step):
            for _way, src_e, present in sources(step):

                @pl.when(present)
                def _():
                    take_other(src_e, part)

    def sum_parts():
        part_copy(0, 1).wait_recv()
        part_own[...] += pltpu.roll(part_recv[0, 1].astype(F32), HD // 2, 1)
        for o in range(1, reach + 1):

            @pl.when(c + o < ctx_size)
            def _():
                part_copy(o, 0).wait_recv()
                part_copy(o, 1).wait_recv()
                part_own[...] += part_recv[o, 0].astype(F32) + pltpu.roll(
                    part_recv[o, 1].astype(F32), HD // 2, 1
                )

        summed = part_own[...].T.astype(BF16)
        dk_out[...] = summed[: HD // 2]
        dv_out[...] = summed[HD // 2 :]

    for step in range(1, experts):
        forward(step + 1, 0)
        arrive(step)
        for k in range(1, chunks):
            forward(step + 1, k)
        arrive_other(step - 1)
        if step == max(1, experts - 2):
            sum_parts()
    arrive_other(experts - 1)

    gate_sum = jnp.sum(gate_acc[...], axis=1, keepdims=True)
    dgate_out[...] = jnp.broadcast_to(gate_sum, (cap, HD)).T[:1]

    y_copy(e, whole[0]).wait_send()
    for k in range(chunks):

        @pl.when(e < experts - 1)
        def _():
            row_copy(0, e, k).wait_send()

        @pl.when(e > 0)
        def _():
            row_copy(1, e, k).wait_send()

    for step in range(1, experts):
        for way, src_e, present in sources(step):

            @pl.when(present)
            def _():
                for part in parts_at(step):
                    y_copy(src_e, part).wait_send()

                @pl.when(e < experts - 1 if way == 0 else e > 0)
                def _():
                    for k in range(chunks):
                        row_copy(way, src_e, k).wait_send()

    part_copy(0, 1).wait_send()
    for o in range(1, reach + 1):

        @pl.when(c + o < ctx_size)
        def _():
            kv_copy(o).wait_send()

        @pl.when(c >= o)
        def _():
            part_copy(o, 0).wait_send()
            part_copy(o, 1).wait_send()


def write(*refs):
    sources, targets, sem = refs[:5], refs[5:10], refs[10]
    copies = [
        pltpu.make_async_copy(source, target, sem.at[i])
        for i, (source, target) in enumerate(zip(sources, targets))
    ]
    for copy in reversed(copies):
        copy.start()
    for copy in copies:
        copy.wait()


def local(
    queries,
    key_rows,
    value_rows,
    out_grad,
    attn_out,
    doc_ids,
    row_grad,
    gate_weights,
    expert_ids,
    expert_out,
):
    ctx_size, tp_size = lax.axis_size("ctx"), lax.axis_size("tp")
    n, width = row_grad.shape
    cap, features = expert_out.shape[1:]
    experts = tp_size // 2
    reach = min((doc_ids.shape[0] // 2 + n) // n, ctx_size - 1)
    chunks = len(cuts(width))
    blocks = reach + 1
    stacked = QH_DEV * n
    dma = pltpu.SemaphoreType.DMA
    out_shape = (
        jax.ShapeDtypeStruct(queries.shape, BF16),
        jax.ShapeDtypeStruct((HD // 2, n), BF16),
        jax.ShapeDtypeStruct((HD // 2, n), BF16),
        jax.ShapeDtypeStruct((1, cap), F32),
        jax.ShapeDtypeStruct(expert_out.shape, BF16),
    )
    outs = pl.pallas_call(
        functools.partial(kernel, ctx_size, tp_size, reach),
        out_shape=tuple(pltpu.VMEM(out.shape, out.dtype) for out in out_shape),
        in_specs=[pl.BlockSpec(memory_space=pltpu.HBM)] * 10,
        out_specs=[pl.BlockSpec(memory_space=pltpu.VMEM)] * 5,
        scratch_shapes=[
            pltpu.VMEM(queries.shape, BF16),
            pltpu.VMEM(queries.shape, BF16),
            pltpu.VMEM(queries.shape, BF16),
            pltpu.VMEM((doc_ids.shape[0] // n, n), jnp.int32),
            pltpu.VMEM(gate_weights.shape[::-1], F32),
            pltpu.VMEM(expert_ids.shape[::-1], jnp.int32),
            pltpu.VMEM((cap, features), BF16),
            pltpu.VMEM((blocks, 2, n, HD), BF16),
            pltpu.VMEM((stacked, HD), BF16),
            pltpu.VMEM((stacked, HD), BF16),
            pltpu.VMEM((stacked, HD), BF16),
            pltpu.VMEM((stacked, HD), BF16),
            pltpu.VMEM((stacked, 1), F32),
            pltpu.VMEM((blocks, stacked, n), F32),
            pltpu.VMEM((stacked, n), F32),
            pltpu.VMEM((stacked, n), F32),
            pltpu.VMEM((stacked, HD), F32),
            pltpu.VMEM((blocks, 2, n, HD), BF16),
            pltpu.VMEM((n, HD), F32),
            pltpu.VMEM((blocks, 2, n, HD), BF16),
            pltpu.VMEM((experts, n, width), BF16),
            pltpu.VMEM((2 * cap, n), BF16),
            pltpu.VMEM((cap, 1), F32),
            pltpu.VMEM((experts, cap, width), BF16),
            pltpu.VMEM((experts, cap, width), BF16),
            pltpu.VMEM((cap, HD), F32),
            dma((9,)),
            dma((chunks,)),
            dma((blocks,)),
            dma((blocks,)),
            dma((blocks, 2)),
            dma((blocks, 2)),
            dma((2, experts, chunks)),
            dma((experts, chunks)),
            dma((experts, chunks)),
            dma((experts, chunks)),
        ],
        compiler_params=pltpu.CompilerParams(
            collective_id=0, has_side_effects=True, vmem_limit_bytes=VMEM
        ),
        name="backward",
    )(
        *(
            pltpu.with_memory_space_constraint(operand, pltpu.HBM)
            for operand in (
                queries,
                key_rows,
                value_rows,
                out_grad,
                attn_out,
                doc_ids.reshape(-1, n),
                row_grad,
                gate_weights.T,
                expert_ids.T,
                expert_out,
            )
        )
    )
    query_grad, key_grad, value_grad, gate_grad, expert_grad = pl.pallas_call(
        write,
        out_shape=out_shape,
        in_specs=[pl.BlockSpec(memory_space=pltpu.VMEM)] * 5,
        out_specs=[pl.BlockSpec(memory_space=pltpu.HBM)] * 5,
        scratch_shapes=[dma((5,))],
        compiler_params=pltpu.CompilerParams(vmem_limit_bytes=8 * 1024 * 1024),
        name="write",
    )(*outs)
    return (query_grad, key_grad.T, value_grad.T, gate_grad, expert_grad)


def solution(mesh):
    in_specs = (
        P("ctx", "tp"),
        P("ctx", None),
        P("ctx", None),
        P("ctx", "tp"),
        P("ctx", "tp"),
        P(),
        P("ctx", "tp"),
        P("ctx", None),
        P("ctx", None),
        P("ctx", "tp", None),
    )
    out_specs = (
        P("ctx", "tp"),
        P("ctx", "tp"),
        P("ctx", "tp"),
        P("ctx", "tp"),
        P("ctx", "tp", None),
    )
    return jax.shard_map(local, mesh=mesh, in_specs=in_specs, out_specs=out_specs, check_vma=False)
```
